32 devices in a mesh: dp: 8 (over z, y), level: 4 (over x, core).
Axes of the slice: x: 2, y: 2, z: 4, core: 2. Of those that a mesh axis runs over, the one named last changes fastest.
Arguments:
- queries: bfloat16 [4800, 256], P('dp'), may hold values from -6 to 6
- memory: bfloat16 [16, 4, 16700, 256], P('dp', 'level'), may hold values from -6 to 6
- frame_size: int32 [16, 2], P('dp'), may hold values from 60 to 167, as said below
- sample_pick: int32 [4800, 4, 64], P('dp', 'level'), may hold values from 0 to 32767
- target_box: float32 [16, 32, 4], P('dp'), as said below
- match: int32 [16, 32], P('dp'), may hold values from 0 to 299, as said below
- obj_count: int32 [16], P('dp'), may hold values from 1 to 32
- w_query: float32 [256, 384], P('dp'), may hold values from -0.375 to 0.375
- w_square: float32 [12, 256, 256], P(None, 'dp')
- w_ffn_in: float32 [2, 256, 1024], P(None, 'dp'), may hold values from -0.375 to 0.375
- w_ffn_out: float32 [2, 1024, 256], P(None, 'dp'), may hold values from -0.1875 to 0.1875
- vectors: float32 [21, 256], P(None, 'dp')
- m_query: float32 [256, 384], P('dp'), may hold values from -0.1875 to 0.1875
- m_square: float32 [12, 256, 256], P(None, 'dp'), may hold values from -0.1875 to 0.1875
- m_ffn_in: float32 [2, 256, 1024], P(None, 'dp'), may hold values from -0.1875 to 0.1875
- m_ffn_out: float32 [2, 1024, 256], P(None, 'dp'), may hold values from -0.1875 to 0.1875
- m_vectors: float32 [21, 256], P(None, 'dp'), may hold values from -0.1875 to 0.1875
- a_query: float32 [256, 384], P('dp'), may hold values from -0.375 to 0.375
- a_square: float32 [12, 256, 256], P(None, 'dp'), may hold values from -0.375 to 0.375
- a_ffn_in: float32 [2, 256, 1024], P(None, 'dp'), may hold values from -0.375 to 0.375
- a_ffn_out: float32 [2, 1024, 256], P(None, 'dp'), may hold values from -0.1875 to 0.1875
- a_vectors: float32 [21, 256], P(None, 'dp'), may hold values from 0.5 to 1.5
Outputs:
- loss_sum: float32 [], replicated
- object_total: float32 [], replicated
- query_weight: float32 [256, 384], P('dp')
- query_copy: bfloat16 [256, 384], P('dp')
- query_moment: float32 [256, 384], P('dp')
- query_average: float32 [256, 384], P('dp')
- square_weight: float32 [12, 256, 256], P(None, 'dp')
- square_copy: bfloat16 [12, 256, 256], P(None, 'dp')
- square_moment: float32 [12, 256, 256], P(None, 'dp')
- square_average: float32 [12, 256, 256], P(None, 'dp')
- ffn_in_weight: float32 [2, 256, 1024], P(None, 'dp')
- ffn_in_copy: bfloat16 [2, 256, 1024], P(None, 'dp')
- ffn_in_moment: float32 [2, 256, 1024], P(None, 'dp')
- ffn_in_average: float32 [2, 256, 1024], P(None, 'dp')
- ffn_out_weight: float32 [2, 1024, 256], P(None, 'dp')
- ffn_out_copy: bfloat16 [2, 1024, 256], P(None, 'dp')
- ffn_out_moment: float32 [2, 1024, 256], P(None, 'dp')
- ffn_out_average: float32 [2, 1024, 256], P(None, 'dp')
- vector_weight: float32 [21, 256], P(None, 'dp')
- vector_copy: bfloat16 [21, 256], P(None, 'dp')
- vector_moment: float32 [21, 256], P(None, 'dp')
- vector_average: float32 [21, 256], P(None, 'dp')
The draws below stay inside these ranges and needn't reach their ends.
Inputs may be any that keep to these rules, and one draw needn't show every extreme that they name: `frame_size`: column 0 is the rows, column 1 the columns of the finest grid; rows lie in 60 to 100, columns in 80 to 167. `match`: distinct queries within a frame. `target_box`: centres lie in 0.2 to 0.8, widths and heights in 0.05 to 0.4.
All inputs are finite; a program needn't handle non-finite values.
Results may differ from the reference program's by a relative error of at most 0.019.
Values may be sent and summed in bfloat16 or wider, within the bound.
No kernel may reach another device: no remote copies, remote signals or barrier semaphores. Data moves between devices by JAX's collectives and lax.ppermute only.
A program may use at most 384 MiB of HBM per device.

```python
import jax
import jax.numpy as jnp
from jax import lax

D = 256
H = 8
NL = 4
P_SIZE = 4
FF = 1024
Q = 300
OBJ = 32
H0 = 100
W0 = 167
H_MIN = 60
W_MIN = 80
MCAP = 16700
FRAMES = 16
TOKENS = 4800


def draw_frame_size(key, part):
    key = jax.random.fold_in(key, 1)
    key_rows, key_cols = jax.random.split(key)
    heights = jax.random.randint(key_rows, (FRAMES,), H_MIN, H0 + 1)
    widths = jax.random.randint(key_cols, (FRAMES,), W_MIN, W0 + 1)
    heights = heights.at[0].set(H0)
    widths = widths.at[0].set(W0)
    return jnp.stack([heights, widths], 1).astype(jnp.int32)


def draw_match(key, part):
    key = jax.random.fold_in(key, 2)
    frame_keys = jax.random.split(key, FRAMES)
    return jax.vmap(lambda single: jax.random.permutation(single, Q)[:OBJ])(frame_keys).astype(jnp.int32)


def draw_obj_count(key, part):
    key = jax.random.fold_in(key, 3)
    frame_ids = jnp.arange(FRAMES, dtype=jnp.int32)
    lowest = max(OBJ // 3, 2)
    ceiling = lowest + (OBJ - lowest) * frame_ids // max(FRAMES - 1, 1)
    counts = jax.random.randint(key, (FRAMES,), 1, ceiling + 1)
    return counts.at[FRAMES - 1].set(OBJ).astype(jnp.int32)


def draw_target_box(key, part):
    key = jax.random.fold_in(key, 4)
    unit_draw = jax.random.uniform(key, (FRAMES, OBJ, 4), jnp.float32)
    lowest = jnp.array([0.2, 0.2, 0.05, 0.05], jnp.float32)
    extent = jnp.array([0.6, 0.6, 0.35, 0.35], jnp.float32)
    return lowest + extent * unit_draw


def draw_w_square(key, part):
    key = jax.random.fold_in(key, 5)
    base_draw = jax.random.normal(key, (12, D, D), jnp.float32)
    factors = jnp.array([1.0, 1.0, 1.0, 4.0, 1.0, 3.0, 1.0, 1.0, 1.0, 4.0, 1.0, 1.0], jnp.float32)
    return base_draw * factors[:, None, None] * D ** (-0.5)


def draw_vectors(key, part):
    key = jax.random.fold_in(key, 6)
    base_draw = jax.random.normal(key, (21, D), jnp.float32)
    row_ids = jnp.arange(21)[:, None]
    gains = 1.0 + 0.1 * base_draw
    shifts = 0.2 * base_draw
    output_rows = base_draw * D ** (-0.5)
    is_gain = (row_ids < 10) & (row_ids % 2 == 0)
    return jnp.where(is_gain, gains, jnp.where(row_ids >= 17, output_rows, shifts))


def plant(entries, key, smallest, top_value):
    longest = entries.shape.index(max(entries.shape))
    spots = []
    for shift in (0, 1):
        where = [jax.random.randint(jax.random.fold_in(key, axis), (), 0, length) for axis, length in enumerate(entries.shape)]
        where[longest] = (where[longest] + shift) % entries.shape[longest]
        spots.append(tuple(where))
    return entries.at[spots[0]].set(smallest).at[spots[1]].set(top_value)


def steps_of(own_key, dims, cuts, least, high):
    level = 1.0
    for dim, shards_of in cuts:
        steps = jax.random.uniform(jax.random.fold_in(jax.random.fold_in(own_key, 6), dim), (shards_of,), jnp.float32, least / len(cuts), high / len(cuts))
        level = level * jnp.repeat(jnp.exp(steps), dims[dim] // shards_of).reshape((-1,) + (1,) * (len(dims) - 1 - dim))
    return level


def gaussian(stream_key, shape, scale, limit, shards=(), kind=jnp.bfloat16):
    values = scale * jax.random.normal(stream_key, shape, jnp.float32)
    if shards:
        values = values * steps_of(stream_key, shape, shards, -0.22, 0.18)
    return jnp.clip(values, -limit, limit).astype(kind)


def setup_inputs(seed: int = 0) -> dict:
    key_of = jax.random.split(jax.random.key(seed), 23)
    queries = gaussian(key_of[0], (TOKENS, D), 1.0, 6.0, ((0, 8),))
    memory = gaussian(key_of[1], (FRAMES, NL, MCAP, D), 1.0, 6.0, ((0, 8), (1, 4)))
    frame_size = draw_frame_size(jax.random.fold_in(key_of[22], 71), 0)
    sample_pick = plant(jax.random.randint(key_of[3], (TOKENS, NL, 2 * H * P_SIZE), 0, 32768), jax.random.fold_in(key_of[3], 1), 0, 32767).astype(jnp.int32)
    target_box = draw_target_box(jax.random.fold_in(key_of[22], 71), 0)
    match = draw_match(jax.random.fold_in(key_of[22], 71), 0)
    obj_count = draw_obj_count(jax.random.fold_in(key_of[22], 71), 0)
    w_query = gaussian(key_of[7], (D, 3 * NL * H * P_SIZE), D ** -0.5, 0.375, ((0, 8),), jnp.float32)
    w_square = draw_w_square(jax.random.fold_in(key_of[22], 71), 0)
    w_ffn_in = gaussian(key_of[9], (2, D, FF), D ** -0.5, 0.375, ((1, 8),), jnp.float32)
    w_ffn_out = gaussian(key_of[10], (2, FF, D), FF ** -0.5, 0.1875, ((1, 8),), jnp.float32)
    vectors = draw_vectors(jax.random.fold_in(key_of[22], 71), 0)
    m_query = gaussian(key_of[12], (D, 3 * NL * H * P_SIZE), (0.3 * (FRAMES * OBJ) ** -0.5), 0.1875, ((0, 8),), jnp.float32)
    m_square = gaussian(key_of[13], (12, D, D), (0.3 * (FRAMES * OBJ) ** -0.5), 0.1875, ((1, 8),), jnp.float32)
    m_ffn_in = gaussian(key_of[14], (2, D, FF), (0.3 * (FRAMES * OBJ) ** -0.5), 0.1875, ((1, 8),), jnp.float32)
    m_ffn_out = gaussian(key_of[15], (2, FF, D), (0.3 * (FRAMES * OBJ) ** -0.5), 0.1875, ((1, 8),), jnp.float32)
    m_vectors = gaussian(key_of[16], (21, D), (0.3 * (FRAMES * OBJ) ** -0.5), 0.1875, ((1, 8),), jnp.float32)
    a_query = gaussian(key_of[17], (D, 3 * NL * H * P_SIZE), D ** -0.5, 0.375, ((0, 8),), jnp.float32)
    a_square = gaussian(key_of[18], (12, D, D), D ** -0.5, 0.375, ((1, 8),), jnp.float32)
    a_ffn_in = gaussian(key_of[19], (2, D, FF), D ** -0.5, 0.375, ((1, 8),), jnp.float32)
    a_ffn_out = gaussian(key_of[20], (2, FF, D), FF ** -0.5, 0.1875, ((1, 8),), jnp.float32)
    a_vectors = jnp.clip(1.0 + 0.1 * jax.random.normal(key_of[21], (21, D), jnp.float32), 0.5, 1.5)
    return dict(queries=queries, memory=memory, frame_size=frame_size, sample_pick=sample_pick, target_box=target_box, match=match, obj_count=obj_count, w_query=w_query, w_square=w_square, w_ffn_in=w_ffn_in, w_ffn_out=w_ffn_out, vectors=vectors, m_query=m_query, m_square=m_square, m_ffn_in=m_ffn_in, m_ffn_out=m_ffn_out, m_vectors=m_vectors, a_query=a_query, a_square=a_square, a_ffn_in=a_ffn_in, a_ffn_out=a_ffn_out, a_vectors=a_vectors)


@jax.custom_vjp
def low(v):
    return lax.optimization_barrier(v.astype(jnp.bfloat16)).astype(jnp.float32)

@jax.custom_vjp
def low_back(v):
    return v

def low_keep(v):
    return (low(v), None)

def low_pass(kept, grad):
    return (grad,)

def back_keep(v):
    return (v, None)

def back_low(kept, grad):
    return (low(grad),)
low.defvjp(low_keep, low_pass)
low_back.defvjp(back_keep, back_low)
HIGHEST = lax.Precision.HIGHEST
LEARNING_RATE = 2.0
MOMENTUM = 0.5
AVERAGING = 0.5
EPSILON = 1e-05
SMOOTHING = 1e-06

def product(left, right):
    return low_back(jnp.dot(left, right, precision=HIGHEST))

def layer_norm(values, gain, shift):
    centred = values - lax.optimization_barrier(jnp.mean(values, -1, keepdims=True))
    spread = lax.optimization_barrier(jnp.mean(centred * centred, -1, keepdims=True))
    return centred * lax.rsqrt(spread + EPSILON) * gain + shift

def attend(inputs, w_four, bias_out, gain, shift):
    rows = inputs.shape[0]
    shaped = low(inputs)

    def heads(weight):
        return low(product(shaped, weight)).reshape(rows // Q, Q, H, D // H)
    query_part, key_part, value_part = (heads(w_four[0]), heads(w_four[1]), heads(w_four[2]))
    scores = low_back(jnp.einsum('fqhe,fkhe->fhqk', query_part, key_part, precision=HIGHEST)) * (D // H) ** (-0.5)
    weights = low(jax.nn.softmax(scores, -1))
    mixed = low(low_back(jnp.einsum('fhqk,fkhe->fqhe', weights, value_part, precision=HIGHEST))).reshape(rows, D)
    return layer_norm(inputs + product(mixed, w_four[3]) + bias_out, gain, shift)

def smooth_max(first, second):
    return 0.5 * (first + second + jnp.sqrt((first - second) ** 2 + SMOOTHING))

def smooth_min(first, second):
    return 0.5 * (first + second - jnp.sqrt((first - second) ** 2 + SMOOTHING))

def box_cost(picked, target):
    differ = picked - target
    distance = lax.optimization_barrier(jnp.sum(jnp.sqrt(differ * differ + 0.01), -1))
    pred_lower = picked[:, :2] - 0.5 * picked[:, 2:]
    pred_upper = picked[:, :2] + 0.5 * picked[:, 2:]
    targ_lower = target[:, :2] - 0.5 * target[:, 2:]
    targ_upper = target[:, :2] + 0.5 * target[:, 2:]
    intersection = smooth_max(smooth_min(pred_upper, targ_upper) - smooth_max(pred_lower, targ_lower), 0.0)
    inter = intersection[:, 0] * intersection[:, 1]
    union = picked[:, 2] * picked[:, 3] + target[:, 2] * target[:, 3] - inter
    enclose = smooth_max(pred_upper, targ_upper) - smooth_min(pred_lower, targ_lower)
    hull = enclose[:, 0] * enclose[:, 1]
    general = inter / union - (hull - union) / hull
    return 5.0 * distance + 2.0 * (1.0 - general)

def post_loss(sampled, resid, w_square, w_in, w_back, vr, pick_rows, targets, valid):
    first = layer_norm(resid + product(sampled, w_square[5]) + vr[11], vr[2], vr[3])
    hidden = low(jax.nn.gelu(product(low(first), w_in[0])))
    second = layer_norm(first + product(hidden, w_back[0]) + vr[12], vr[4], vr[5])
    third = attend(second, w_square[6:10], vr[13], vr[6], vr[7])
    hidden_two = low(jax.nn.gelu(product(low(third), w_in[1])))
    fourth = layer_norm(third + product(hidden_two, w_back[1]) + vr[14], vr[8], vr[9])
    box_one = low(jax.nn.gelu(product(low(fourth), w_square[10]) + vr[15]))
    box_two = low(jax.nn.gelu(product(box_one, w_square[11]) + vr[16]))
    boxes = jax.nn.sigmoid(product(box_two, jnp.transpose(vr[17:21])))
    picked = jnp.take(boxes, pick_rows, axis=0)
    return jnp.sum(valid * box_cost(picked, targets))

def corner_data(frame_size, picked_cells, stride):
    row_count = picked_cells.shape[0]
    frame_of = jnp.arange(row_count, dtype=jnp.int32) // Q
    heights = ((frame_size[:, 0] + stride - 1) // stride)[frame_of][:, None]
    widths = ((frame_size[:, 1] + stride - 1) // stride)[frame_of][:, None]
    top_row = picked_cells[:, :H * P_SIZE] % jnp.maximum(heights - 1, 1)
    leftmost = picked_cells[:, H * P_SIZE:] % jnp.maximum(widths - 1, 1)
    bottom = jnp.minimum(top_row + 1, heights - 1)
    rightmost = jnp.minimum(leftmost + 1, widths - 1)
    return jnp.stack([top_row * widths + leftmost, top_row * widths + rightmost, bottom * widths + leftmost, bottom * widths + rightmost], -1)

def combine(gathered, frac_x, frac_y, weights):
    corner_weight = jnp.stack([(1.0 - frac_y) * (1.0 - frac_x), (1.0 - frac_y) * frac_x, frac_y * (1.0 - frac_x), frac_y * frac_x], -1)
    coefs = weights[..., None] * corner_weight
    pieces = lax.optimization_barrier(jnp.sum(coefs[..., None] * gathered, 2))
    row_count = pieces.shape[0]
    return lax.optimization_barrier(jnp.sum(pieces.reshape(row_count, H, P_SIZE, -1), 2)).reshape(row_count, -1)

def sample_frame(value_proj, memory_frame, corners, frac_x, frac_y, attention):
    values = low(low_back(jnp.einsum('lmd,de->lme', memory_frame.astype(jnp.float32), value_proj, precision=HIGHEST)))
    values = values.reshape(NL, MCAP * H, D // H)
    head_of = (jnp.arange(H * P_SIZE, dtype=jnp.int32) // P_SIZE)[None, :, None]
    summed = jnp.zeros((Q, D), jnp.float32)
    for pyramid in range(NL):
        gathered = values[pyramid][corners[pyramid] * H + head_of]
        summed = summed + combine(gathered, frac_x[:, pyramid], frac_y[:, pyramid], attention[:, pyramid])
    return summed

def forward(w_query, w_square, w_ffn_in, w_ffn_out, vr, queries, memory, corners, pick_rows, targets, valid):
    decoded = attend(queries, w_square[0:4], vr[10], vr[0], vr[1])
    projected = product(low(decoded), w_query)
    columns = NL * H * P_SIZE
    frac_x = jax.nn.sigmoid(projected[:, :columns]).reshape(FRAMES, Q, NL, H * P_SIZE)
    frac_y = jax.nn.sigmoid(projected[:, columns:2 * columns]).reshape(FRAMES, Q, NL, H * P_SIZE)
    logits = projected[:, 2 * columns:].reshape(TOKENS, NL, H, P_SIZE).transpose(0, 2, 1, 3).reshape(TOKENS, H, NL * P_SIZE)
    attention = jax.nn.softmax(logits, -1).reshape(TOKENS, H, NL, P_SIZE).transpose(0, 2, 1, 3).reshape(FRAMES, Q, NL, H * P_SIZE)

    def frame_step(state_carry, inputs):
        return (state_carry, sample_frame(w_square[4], *inputs))
    unused, sampled = lax.scan(jax.checkpoint(frame_step), jnp.float32(0.0), (memory, corners, frac_x, frac_y, attention))
    sampled = low(low_back(sampled.reshape(TOKENS, D)))
    return post_loss(sampled, decoded, w_square, w_ffn_in, w_ffn_out, vr, pick_rows, targets, valid)

def update(master, gradient, moment, average):
    moment_new = MOMENTUM * moment + gradient
    master_new = master - LEARNING_RATE * (gradient + MOMENTUM * moment_new)
    average_new = AVERAGING * average + (1.0 - AVERAGING) * master_new
    return (master_new, master_new.astype(jnp.bfloat16), moment_new, average_new)

def reference(queries, memory, frame_size, sample_pick, target_box, match, obj_count, w_query, w_square, w_ffn_in, w_ffn_out, vectors, m_query, m_square, m_ffn_in, m_ffn_out, m_vectors, a_query, a_square, a_ffn_in, a_ffn_out, a_vectors):
    masters = (w_query, w_square, w_ffn_in, w_ffn_out, vectors)
    copies = tuple((lax.optimization_barrier(weight.astype(jnp.bfloat16)).astype(jnp.float32) for weight in masters))
    corners = jnp.stack([corner_data(frame_size, sample_pick[:, pyramid], 2 ** pyramid) for pyramid in range(NL)], 1)
    corners = corners.reshape(FRAMES, Q, NL, H * P_SIZE, 4).transpose(0, 2, 1, 3, 4)
    object_total = jnp.sum(obj_count).astype(jnp.float32)
    pick_rows = (jnp.arange(FRAMES, dtype=jnp.int32)[:, None] * Q + match).reshape(-1)
    valid = (jnp.arange(OBJ, dtype=jnp.int32)[None, :] < obj_count[:, None]).astype(jnp.float32).reshape(-1)
    targets = target_box.reshape(-1, 4)
    inputs = queries.astype(jnp.float32)

    def loss_of(*weights):
        return forward(*weights, inputs, memory, corners, pick_rows, targets, valid)
    loss_sum, backward = jax.vjp(loss_of, *copies)
    grads = backward(jnp.float32(1.0) / object_total)
    moments = (m_query, m_square, m_ffn_in, m_ffn_out, m_vectors)
    averages = (a_query, a_square, a_ffn_in, a_ffn_out, a_vectors)
    results = [update(masters[k], grads[k], moments[k], averages[k]) for k in range(5)]
    return (loss_sum, object_total, results[0][0], results[0][1], results[0][2], results[0][3], results[1][0], results[1][1], results[1][2], results[1][3], results[2][0], results[2][1], results[2][2], results[2][3], results[3][0], results[3][1], results[3][2], results[3][3], results[4][0], results[4][1], results[4][2], results[4][3])
```

```python
import jax
import jax.numpy as jnp
from jax import lax
from jax.experimental import pallas as pl
from jax.experimental.pallas import tpu as pltpu
from jax.sharding import PartitionSpec as P

D = 256
H = 8
P_SIZE = 4
Q = 300
MCAP = 16700
FR = 304
R = 2 * FR
NB = R // 4
PAD = 8
STRIDE = 168
ROWS = 100
TABLE = PAD + (ROWS + 1) * STRIDE + PAD
STAGE = 19
COPIES = 4
SHARDS = 8
RS = D // SHARDS
EARLY_BITS = (4, 2, 1)
LATE_BITS = (1, 2, 4)
BF = jnp.bfloat16
F32 = jnp.float32
VMEM_LIMIT = 62 * 1024 * 1024


def lane_iota(rows):
    return lax.broadcasted_iota(jnp.int32, (rows, 128), 1)


def dot(a, b):
    return jnp.dot(a, b, preferred_element_type=F32)


def dot_nt(a, b):
    return lax.dot_general(a, b, (((1,), (1,)), ((), ())), preferred_element_type=F32)


def dot_tn(a, b):
    return lax.dot_general(a, b, (((0,), (0,)), ((), ())), preferred_element_type=F32)


def expand_matrix(point, dy):
    row = lax.broadcasted_iota(jnp.int32, (128, 256), 0)
    col = lax.broadcasted_iota(jnp.int32, (128, 256), 1) // 32
    return (row == dy * 32 + col * 4 + point).astype(F32).astype(BF)


def fold_matrix(point):
    row = lax.broadcasted_iota(jnp.int32, (256, 128), 0) // 32
    col = lax.broadcasted_iota(jnp.int32, (256, 128), 1)
    return (col == row * 4 + point).astype(F32).astype(BF)


def join_frames(own, mine_ref, other_ref, scr):
    scr[own] = mine_ref[...]
    scr[1 - own] = other_ref[...]
    return scr[...].reshape(R, scr.shape[-1])


def place_coefs(fa, scr):
    lane = lane_iota(R)
    low = lane < 32
    r32, r64, r96 = pltpu.roll(fa, 32, 1), pltpu.roll(fa, 64, 1), pltpu.roll(fa, 96, 1)
    fx = jnp.where(low, fa, r32)
    cy = jnp.where(low, 1.0 - r96, fa)
    att = jnp.where(low, r64, r96)
    base = jnp.where(lane < 64, att * cy, 0.0)
    for dx in range(2):
        coef = base * (fx if dx else 1.0 - fx)
        for k in range(4):
            scr[pl.ds(2 * k + dx, NB, 8), :] = coef[k * NB : (k + 1) * NB]


def fill_weights(scr, wexp):
    packed = scr[...].astype(BF)
    for point in range(4):
        for dy in range(2):
            wexp[point * 2 + dy] = dot(packed, expand_matrix(point, dy)).astype(wexp.dtype)


def row_masks():
    lane = lane_iota(8) // 32
    sub = lax.broadcasted_iota(jnp.int32, (8, 128), 0)
    heads = [lane == h for h in range(4)]
    rows = [sub // 2 == k for k in range(4)]
    return heads, rows


def pick_copies(idx_ref, picks, sem):
    return [pltpu.make_async_copy(idx_ref.at[c % 4, c // 4], picks[c], sem) for c in range(128)]


class Chunks:
    def __init__(self, mem_ref, buf, stage, sems, size_ref, ids_ref):
        self.mem_ref, self.buf, self.stage, self.sems = mem_ref, buf, stage, sems
        self.cells = buf.shape[1]
        level = ids_ref[0]
        self.high, self.wide = (
            [(size_ref[f, axis] + (1 << level) - 1) >> level for f in range(2)] for axis in range(2)
        )
        used = jnp.maximum(self.high[0] * self.wide[0], self.high[1] * self.wide[1])
        self.count = lax.div(used + self.cells - 1, self.cells)
        self.inner = slice(2 * STRIDE, 2 * STRIDE + 2 * self.cells)
        self.whole = -(-MCAP // self.cells)
        self.again = self.whole * self.cells - MCAP

    def base(self, j):
        return jnp.minimum(j * self.cells, MCAP - self.cells)

    def grid_rows(self, cell, f):
        return lax.div(jnp.minimum(cell, MCAP), self.wide[f])

    def copies(self, j, slot):
        size = self.cells // COPIES
        return [
            pltpu.make_async_copy(
                self.mem_ref.at[0, pl.ds(self.base(j) + c * size, size)],
                self.buf.at[slot, pl.ds(c * size, size)],
                self.sems.at[slot, c],
            )
            for c in range(COPIES)
        ]

    def start(self, j, slot):
        for copy in self.copies(j, slot):
            copy.start()

    def staged(self, i, f, j):
        return pl.ds(2 * (i * self.wide[f] - self.base(j) + STRIDE) + f, STRIDE, 2)

    def run(self, work):
        def body(j, carry):
            slot = j % 2

            @pl.when(j + 1 < self.count)
            def _():
                self.start(j + 1, 1 - slot)

            for copy in self.copies(j, slot):
                copy.wait()
            work(j, self.buf[slot].reshape(2 * self.cells, D))
            return carry

        lax.fori_loop(0, self.count, body, 0)


def grid_row(i):
    return pl.ds(pl.multiple_of(i * STRIDE, 8) + PAD, STRIDE)


def pick_kernel(size_ref, ids_ref, pick_ref, out_ref):
    level = ids_ref[0]
    frame = lax.broadcasted_iota(jnp.int32, (1, 2 * Q), 1) >= Q

    def of_frame(column):
        first, second = ((size_ref[f, column] + (1 << level) - 1) >> level for f in range(2))
        return jnp.where(frame, second, first).astype(F32)

    def rest(values, most):
        m = jnp.maximum(most - 1.0, 1.0)
        left = values - jnp.floor(values * (1.0 / m)) * m
        left = jnp.where(left < 0.0, left + m, left)
        return jnp.where(left >= m, left - m, left)

    picks = pick_ref[...].astype(F32)
    cell = rest(picks[:32], of_frame(0)) * STRIDE + rest(picks[32:], of_frame(1))
    row = cell.astype(jnp.int32)
    for k in range(4):
        first = (k // 2) * Q + (k % 2) * NB
        width = NB if k % 2 == 0 else Q - NB
        out_ref[k, :, :width] = row[:, first : first + width]
        if width < NB:
            out_ref[k, :, width:] = jnp.zeros((32, NB - width), jnp.int32)


def pick_rows(size, ids, picks):
    return pl.pallas_call(
        pick_kernel,
        in_specs=[SM, SM, VM],
        out_specs=VM,
        out_shape=jax.ShapeDtypeStruct((4, 32, NB), jnp.int32),
        name="pick_rows",
    )(size, ids, picks)


def forward_kernel(
    idx_ref, size_ref, ids_ref, mem_ref, s4_ref, mine_ref, other_ref,
    g_ref, out_ref, send_ref,
    buf, stage, tables, wexp, racc, cscr, fscr, gscr, gtmp, sems, isem, gsems, *picks,
):
    own = ids_ref[1]
    chunks = Chunks(mem_ref, buf, stage, sems, size_ref, ids_ref)
    chunks.start(0, 0)
    for copy in pick_copies(idx_ref, picks, isem):
        copy.start()
    place_coefs(join_frames(own, mine_ref, other_ref, fscr), cscr)
    fill_weights(cscr, wexp)

    def fill(j, m):
        v = dot(m, s4_ref[...])
        for half in range(2):
            stage[half, chunks.inner, :] = v[:, half * 128 : half * 128 + 128]
        for f in range(2):
            first = chunks.grid_rows(j * chunks.cells, f)
            last = jnp.minimum(chunks.grid_rows((j + 1) * chunks.cells, f), chunks.high[f])

            def copy_row(i, carry):
                for half in range(2):
                    tables[f][half][grid_row(i), :] = stage[half, chunks.staged(i, f, j), :]
                return carry

            lax.fori_loop(first, last, copy_row, 0)
        for half in range(2):
            kept = pl.ds(2 * (chunks.base(j + 1) - chunks.base(j)), 2 * STRIDE)
            stage[half, : 2 * STRIDE, :] = stage[half, kept, :]

    chunks.run(fill)
    for copy in pick_copies(idx_ref, picks, isem):
        copy.wait()
    heads, rows = row_masks()

    def block(j):
        found = [None] * 16
        for half in range(2):
            for point in range(4):
                acc = None
                for h in range(4):
                    part = None
                    for k in range(4):
                        r = picks[((half * 4 + h) * 4 + point) * 4 + k][j] + (PAD - 2 * k)
                        table = tables[k // 2][half]
                        new = (table[pl.ds(r, 8), :], table[pl.ds(r + STRIDE, 8), :])
                        part = new if part is None else [jnp.where(rows[k], x, y) for x, y in zip(new, part)]
                    acc = part if acc is None else [jnp.where(heads[h], x, y) for x, y in zip(part, acc)]
                found[half * 8 + point * 2], found[half * 8 + point * 2 + 1] = acc
        return found

    def gather_block(j, carry):
        low = pl.ds(pl.multiple_of((j % 2) * 8, 8), 8)
        for n, found in enumerate(block(j)):
            gtmp[n, low, :] = found
        return carry

    def gather(i, carry):
        lax.fori_loop(2 * i, 2 * i + 2, gather_block, 0)
        at = pl.ds(pl.multiple_of(i * 16, 16), 16)
        for half in range(2):
            lanes = slice(half * 128, half * 128 + 128)
            total = None
            for pd in range(8):
                g = gtmp[half * 8 + pd]
                gscr[pd, at, lanes] = g.astype(BF)
                v = g * wexp[pd, at, lanes].astype(F32)
                total = v if total is None else total + v
            racc[half, at, :] = total
        return carry

    def keep(stage):
        at = pl.ds(pl.multiple_of(stage * STAGE * 16, 16), STAGE * 16)
        return pltpu.make_async_copy(gscr.at[:, at], g_ref.at[:, at], gsems.at[stage])

    def gather_stage(stage, carry):
        lax.fori_loop(stage * STAGE, (stage + 1) * STAGE, gather, 0)
        keep(stage).start()
        return carry

    lax.fori_loop(0, NB // 2 // STAGE, gather_stage, 0)
    for half in range(2):
        a = racc.at[half]
        lanes = slice(half * 128, half * 128 + 128)
        for k in range(2):
            at = slice(k * NB, (k + 1) * NB)
            first, second = (
                (a[pl.ds(2 * n, NB, 8), :] + a[pl.ds(2 * n + 1, NB, 8), :]).astype(BF) for n in (k, k + 2)
            )
            out_ref[at, lanes] = jnp.where(own == 0, first, second)
            send_ref[at, lanes] = jnp.where(own == 0, second, first)
    for stage in range(NB // 2 // STAGE):
        keep(stage).wait()


ANY = pl.BlockSpec(memory_space=pl.ANY)
SM = pl.BlockSpec(memory_space=pltpu.SMEM)
VM = pl.BlockSpec(memory_space=pltpu.VMEM)


def sampling_scratch(cells):
    return [
        pltpu.VMEM((2, cells, 2, D), BF),
        pltpu.VMEM((2, 2 * (cells + 2 * STRIDE), 128), F32),
        [[pltpu.VMEM((TABLE, 128), F32)] * 2] * 2,
        pltpu.VMEM((8, 2 * R, D), BF),
        pltpu.VMEM((2, 2 * R, 128), F32),
        pltpu.VMEM((2 * R, 128), F32),
        pltpu.VMEM((2, FR, 128), F32),
    ]


def sampling_semaphores():
    return [pltpu.SemaphoreType.DMA((2, COPIES)), pltpu.SemaphoreType.DMA(())]


def pick_scratch():
    return [pltpu.SMEM((NB,), jnp.int32)] * 128


def params(limit=VMEM_LIMIT):
    return pltpu.CompilerParams(vmem_limit_bytes=limit)


def cost(flops, moved):
    return pl.CostEstimate(flops=flops, bytes_accessed=moved, transcendentals=0)


def sample_forward(idx, size, ids, memory_t, s4, fa_mine, fa_other):
    frame = jax.ShapeDtypeStruct((FR, D), BF)
    return pl.pallas_call(
        forward_kernel,
        in_specs=[ANY, SM, SM, ANY, VM, VM, VM],
        out_specs=[ANY, VM, VM],
        out_shape=[jax.ShapeDtypeStruct((8, 2 * R, D), BF), frame, frame],
        scratch_shapes=sampling_scratch(1680)
        + [pltpu.VMEM((8, 2 * R, D), BF), pltpu.VMEM((16, 16, 128), F32)]
        + sampling_semaphores()
        + [pltpu.SemaphoreType.DMA((NB // 2 // STAGE,))]
        + pick_scratch(),
        compiler_params=params(),
        cost_estimate=cost(30_000_000_000, 60_000_000),
        name="sample_forward",
    )(idx, size, ids, memory_t, s4, fa_mine, fa_other)


def place_grads(ds, g2):
    ds = ds.astype(F32)
    for half in range(2):
        for k in range(4):
            piece = ds[k * NB : (k + 1) * NB, half * 128 : half * 128 + 128]
            for dx in range(2):
                g2[half, pl.ds(2 * k + dx, NB, 8), :] = piece


def coef_kernel(
    ids_ref, g_ref, ds_mine, ds_other, fa_mine, fa_other, out_ref, send_ref, g2, scr, dscr, fscr
):
    own = ids_ref[1]
    place_grads(join_frames(own, ds_mine, ds_other, dscr), g2)
    fa_all = join_frames(own, fa_mine, fa_other, fscr)
    fold = [fold_matrix(point) for point in range(4)]
    for dy in range(2):
        total = None
        for point in range(4):
            for half in range(2):
                lanes = slice(half * 128, half * 128 + 128)
                v = (g_ref[point * 2 + dy, :, lanes].astype(F32) * g2[half]).astype(BF)
                v = dot(v, fold[point][half * 128 : half * 128 + 128])
                total = v if total is None else total + v
        scr[dy] = total
    lane = lane_iota(NB)
    results = []
    for k in range(4):
        at = slice(k * NB, (k + 1) * NB)
        g = [[scr[dy, pl.ds(2 * k + dx, NB, 8), :] for dx in range(2)] for dy in range(2)]
        fa = fa_all[at]
        fx, fy, att = fa, pltpu.roll(fa, 96, 1), pltpu.roll(fa, 64, 1)
        top = (1.0 - fx) * g[0][0] + fx * g[0][1]
        bottom = (1.0 - fx) * g[1][0] + fx * g[1][1]
        d_att = (1.0 - fy) * top + fy * bottom
        d_fy = att * (bottom - top)
        d_fx = att * ((1.0 - fy) * (g[0][1] - g[0][0]) + fy * (g[1][1] - g[1][0]))
        gx = d_fx * fx * (1.0 - fx)
        gy = pltpu.roll(d_fy * fy * (1.0 - fy), 32, 1)
        weighted = pltpu.roll(att * d_att, 64, 1)
        res = jnp.where(lane < 32, gx, jnp.where(lane < 64, gy, jnp.where(lane < 96, weighted, 0.0)))
        results.append(res.astype(BF))
    for k in range(2):
        at = slice(k * NB, (k + 1) * NB)
        out_ref[at] = jnp.where(own == 0, results[k], results[k + 2])
        send_ref[at] = jnp.where(own == 0, results[k + 2], results[k])


def coef_backward(ids, gathered, ds_mine, ds_other, fa_mine, fa_other):
    frame = jax.ShapeDtypeStruct((FR, 128), BF)
    return pl.pallas_call(
        coef_kernel,
        in_specs=[SM] + [VM] * 5,
        out_specs=[VM, VM],
        out_shape=[frame, frame],
        scratch_shapes=[
            pltpu.VMEM((2, 2 * R, 128), F32),
            pltpu.VMEM((2, 2 * R, 128), F32),
            pltpu.VMEM((2, FR, D), BF),
            pltpu.VMEM((2, FR, 128), F32),
        ],
        compiler_params=params(32 * 1024 * 1024),
        cost_estimate=cost(2_000_000_000, 10_000_000),
        name="coef_backward",
    )(ids, gathered, ds_mine, ds_other, fa_mine, fa_other)


def scatter_kernel(
    idx_ref, size_ref, ids_ref, mem_ref, ds_mine, ds_other, fa_mine, fa_other,
    out_ref,
    buf, stage, tables, wexp, g2, cscr, fscr, dscr, sems, isem, sum_ref, *picks,
):
    own = ids_ref[1]
    chunks = Chunks(mem_ref, buf, stage, sems, size_ref, ids_ref)
    for copy in pick_copies(idx_ref, picks, isem):
        copy.start()
    chunks.start(0, 0)
    place_coefs(join_frames(own, fa_mine, fa_other, fscr), cscr)
    fill_weights(cscr, wexp)
    place_grads(join_frames(own, ds_mine, ds_other, dscr), g2)
    for pair in tables:
        for table in pair:
            table[:PAD, :] = jnp.zeros((PAD, 128), F32)
            table[TABLE - PAD :, :] = jnp.zeros((PAD, 128), F32)

    def clear(i, carry):
        for pair in tables:
            for table in pair:
                table[grid_row(i), :] = jnp.zeros((STRIDE, 128), F32)
        return carry

    lax.fori_loop(0, ROWS + 1, clear, 0)
    for copy in pick_copies(idx_ref, picks, isem):
        copy.wait()
    heads, rows = row_masks()

    def scatter(i, carry):
        at = pl.ds(pl.multiple_of(i * 16, 16), 16)
        for point in range(4):
            terms = [
                [wexp[point * 2 + dy, at, half * 128 : half * 128 + 128].astype(F32) * g2[half, at, :] for dy in range(2)]
                for half in range(2)
            ]
            for b in range(2):
                for low in range(2):
                    for half in range(2):
                        todo = []
                        for k in (low, low + 2):
                            for h in range(4):
                                r = picks[((half * 4 + h) * 4 + point) * 4 + k][2 * i + b] + (PAD - 2 * k)
                                table = tables[k // 2][half]
                                for dy in range(2):
                                    spot = pl.ds(r + dy * STRIDE, 8)
                                    value = table[spot, :] + terms[half][dy][8 * b : 8 * b + 8]
                                    todo.append((table, spot, value, heads[h] & rows[k]))
                        for table, spot, value, mask in todo:
                            pltpu.store(table.at[spot, :], value, mask=mask)
        return carry

    lax.fori_loop(0, NB // 2, scatter, 0)
    sum_ref[...] = jnp.zeros((D, D), F32)

    def reduce(j, m):
        for f in range(2):
            first = chunks.grid_rows(j * chunks.cells, f)
            last = chunks.grid_rows(jnp.minimum((j + 1) * chunks.cells, MCAP) - 1, f) + 1

            def copy_row(i, carry):
                at = grid_row(jnp.where(i < chunks.high[f], i, ROWS))
                for half in range(2):
                    stage[half, chunks.staged(i, f, j), :] = tables[f][half][at, :]
                return carry

            lax.fori_loop(first, last, copy_row, 0)
        if chunks.again:

            @pl.when(j == chunks.whole - 1)
            def _():
                stage[:, 2 * STRIDE : 2 * (STRIDE + chunks.again), :] = jnp.zeros((2, 2 * chunks.again, 128), F32)

        g = jnp.concatenate([stage[half, chunks.inner, :].astype(BF) for half in range(2)], 1)
        sum_ref[...] += dot_tn(m, g)

    chunks.run(reduce)
    for n in range(SHARDS):
        out_ref[ids_ref[2] ^ n] = sum_ref[n * RS : (n + 1) * RS].astype(BF)


def sample_backward(idx, size, ids, memory_t, ds_mine, ds_other, fa_mine, fa_other):
    return pl.pallas_call(
        scatter_kernel,
        in_specs=[ANY, SM, SM, ANY] + [VM] * 4,
        out_specs=VM,
        out_shape=jax.ShapeDtypeStruct((SHARDS, RS, D), BF),
        scratch_shapes=sampling_scratch(3344) + [pltpu.VMEM((2, FR, D), BF)] + sampling_semaphores() + [pltpu.VMEM((D, D), F32)] + pick_scratch(),
        compiler_params=params(),
        cost_estimate=cost(30_000_000_000, 60_000_000),
        name="sample_backward",
    )(idx, size, ids, memory_t, ds_mine, ds_other, fa_mine, fa_other)
EPSILON = 1e-05
SMOOTHING = 1e-06
SCALE = (D // H) ** (-0.5)
GELU_C = 0.7978845608028654
GELU_K = 0.044715


def norm_forward(y, gain, shift):
    centred = y - jnp.mean(y, -1, keepdims=True)
    rstd = lax.rsqrt(jnp.mean(centred * centred, -1, keepdims=True) + EPSILON)
    unit = centred * rstd
    return unit * gain + shift, unit, rstd


def norm_backward(grad, unit, rstd, gain):
    d_gain = jnp.sum(grad * unit, 0, keepdims=True)
    d_shift = jnp.sum(grad, 0, keepdims=True)
    g = grad * gain
    dy = rstd * (g - jnp.mean(g, -1, keepdims=True) - unit * jnp.mean(g * unit, -1, keepdims=True))
    return dy, d_gain, d_shift


def gelu_pair(u):
    sq = u * u
    t = jnp.tanh(GELU_C * (u + GELU_K * u * sq))
    half = 0.5 * (1.0 + t)
    slope = half + 0.5 * u * (1.0 - t * t) * (GELU_C * (1.0 + 3.0 * GELU_K * sq))
    return u * half, slope


def head_rows():
    lane = lax.broadcasted_iota(jnp.int32, (1, D), 1) // (D // H)
    return [(lane == h).astype(F32).astype(BF) for h in range(H)]


def attend_forward(x, wq, wk, wv, wo, bias, p_ref):
    xb = x.astype(BF)
    q, k, v = (dot(xb, w).astype(BF) for w in (wq, wk, wv))
    live = lax.broadcasted_iota(jnp.int32, (FR, FR), 1) < Q
    mixed = None
    for h, mask in enumerate(head_rows()):
        s = jnp.where(live, dot_nt(q * mask, k) * SCALE, -1e30)
        e = jnp.exp(s - jnp.max(s, -1, keepdims=True))
        weights = (e / jnp.sum(e, -1, keepdims=True)).astype(BF)
        p_ref[h] = weights
        part = dot(weights, v * mask)
        mixed = part if mixed is None else mixed + part
    mixed = mixed.astype(BF)
    return x + dot(mixed, wo) + bias, xb, q, k, v, mixed


def attend_backward(dy, xb, q, k, v, mixed, p_ref, wq, wk, wv, wo):
    dyb = dy.astype(BF)
    d_wo = dot_tn(mixed, dyb)
    d_mixed = dot_nt(dyb, wo).astype(BF)
    dq = dk = dv = None
    for h, mask in enumerate(head_rows()):
        weights = p_ref[h]
        dm = d_mixed * mask
        dp = dot_nt(dm, v)
        w32 = weights.astype(F32)
        prod = w32 * dp
        ds = ((prod - w32 * jnp.sum(prod, -1, keepdims=True)) * SCALE).astype(BF)
        parts = (dot(ds, k * mask), dot_tn(ds, q * mask), dot_tn(weights, dm))
        dq, dk, dv = parts if dq is None else (dq + parts[0], dk + parts[1], dv + parts[2])
    dq, dk, dv = dq.astype(BF), dk.astype(BF), dv.astype(BF)
    dx = dy + dot_nt(dq, wq) + dot_nt(dk, wk) + dot_nt(dv, wv)
    return dx, (dot_tn(xb, dq), dot_tn(xb, dk), dot_tn(xb, dv), d_wo)


def group_spread(x, op):
    lane = lane_iota(x.shape[0])
    x = op(x, pltpu.roll(x, 64, 1))
    x = op(x, pltpu.roll(x, 32, 1))
    for step in (1, 2):
        other = jnp.where((lane & step) == 0, pltpu.roll(x, 128 - step, 1), pltpu.roll(x, step, 1))
        x = op(x, other)
    return x


def order(bits):
    return [sum(bit for i, bit in enumerate(bits) if n >> i & 1) for n in range(SHARDS)]


def unpack_early(me, own, mine_ref, other_ref, w_ref, wq_ref, s4_ref, vec_ref):
    def take(first_ref, second_ref):
        rows = jnp.zeros((24, D), F32)
        for n in range(SHARDS):
            at = pl.ds(pl.multiple_of((me ^ order(EARLY_BITS)[n]) * RS, RS), RS)
            for m in range(4):
                w_ref[m, at, :] = first_ref[n, m * RS : (m + 1) * RS]
            s4_ref[at, :] = second_ref[n, :RS]
            wq_ref[at, :D] = second_ref[n, RS : 2 * RS]
            right = second_ref[n, 2 * RS : 2 * RS + RS // 2]
            wq_ref[at, D:] = jnp.concatenate([right[:, :128], right[:, 128:]], 0)
            rows = rows + second_ref[n, 2 * RS + RS // 2 : 128].astype(F32)[:24]
        vec_ref[...] = rows

    @pl.when(own == 0)
    def _():
        take(mine_ref, other_ref)

    @pl.when(own == 1)
    def _():
        take(other_ref, mine_ref)


def front_kernel(
    ids_ref, x_ref, mine_ref, other_ref,
    w_ref, wq_ref, s4_ref, vec_ref, total_ref, dec_ref, y_ref, q_ref, k_ref, v_ref, m_ref, p_ref, fa_ref, send_ref, att_ref,
):
    unpack_early(ids_ref[2], ids_ref[1], mine_ref, other_ref, w_ref, wq_ref, s4_ref, vec_ref)
    total_ref[...] = jnp.sum(vec_ref[21:22], -1, keepdims=True) / RS
    x = jnp.concatenate([x_ref[...].astype(F32), jnp.zeros((FR - Q, D), F32)], 0)
    y, _, q, k, v, mixed = attend_forward(x, w_ref[0], w_ref[1], w_ref[2], w_ref[3], vec_ref[10:11], p_ref)
    y_ref[...], q_ref[...], k_ref[...], v_ref[...], m_ref[...] = y, q, k, v, mixed
    dec, _, _ = norm_forward(y, vec_ref[0:1], vec_ref[1:2])
    dec_ref[...] = dec
    proj = dot(dec.astype(BF), wq_ref[...])
    fx, fy = jax.nn.sigmoid(proj[:, :128]), jax.nn.sigmoid(proj[:, 128:256])
    logits = proj[:, 256:]
    e = jnp.exp(logits - group_spread(logits, jnp.maximum))
    att = e / group_spread(e, jnp.add)
    att_ref[...] = att
    lane = lane_iota(FR)
    for out, back in ((fa_ref, ids_ref[0] * 32), (send_ref, (ids_ref[0] ^ 1) * 32)):
        out[...] = jnp.where(
            lane < 32,
            pltpu.roll(fx, 128 - back, 1),
            jnp.where(lane < 64, pltpu.roll(fy, 160 - back, 1), pltpu.roll(att, 192 - back, 1)),
        )


def frame_rows(dt, width=D):
    return jax.ShapeDtypeStruct((FR, width), dt)


WEIGHT_SHAPES = [
    jax.ShapeDtypeStruct((4, D, D), BF),
    jax.ShapeDtypeStruct((D, 384), BF),
    jax.ShapeDtypeStruct((D, D), BF),
    jax.ShapeDtypeStruct((24, D), F32),
    jax.ShapeDtypeStruct((1, 1), F32),
]
DENSE_LIMIT = 40 * 1024 * 1024


def front_forward(ids, x, mine, other):
    return pl.pallas_call(
        front_kernel,
        in_specs=[SM, VM, VM, VM],
        out_specs=[VM] * 15,
        out_shape=WEIGHT_SHAPES
        + [frame_rows(F32)] * 2
        + [frame_rows(BF)] * 4
        + [jax.ShapeDtypeStruct((H, FR, FR), BF)]
        + [frame_rows(F32, 128)] * 3,
        compiler_params=params(),
        cost_estimate=cost(1_000_000_000, 5_000_000),
        name="front_forward",
    )(ids, x, mine, other)


def front_back_kernel(
    ids_ref, near_ref, far_ref, att_ref, dres_ref, x_ref, dec_ref, y_ref, q_ref, k_ref, v_ref, m_ref, p_ref,
    w_ref, wq_ref, vec_ref, dpost_ref,
    mine_ref, send_ref, all_ref,
):
    me, own, level = ids_ref[2], ids_ref[1], ids_ref[0]
    lane = lane_iota(FR)
    cols = [None, None, None]
    for n, gp_ref in enumerate((near_ref.at[0], near_ref.at[1], far_ref.at[0], far_ref.at[1])):
        at = level ^ n
        gp = gp_ref[...].astype(F32)
        here = lane // 32 == at
        for part in range(3):
            piece = jnp.where(here, pltpu.roll(gp, (at + 4 - part) % 4 * 32, 1), 0.0)
            cols[part] = piece if cols[part] is None else cols[part] + piece
    weighted = cols[2]
    cols[2] = weighted - att_ref[...] * group_spread(weighted, jnp.add)
    grad = jnp.concatenate([c.astype(BF) for c in cols], 1)
    d_dec = dres_ref[...] + dot_nt(grad, wq_ref[...])
    _, unit, rstd = norm_forward(y_ref[...], vec_ref[0:1], vec_ref[1:2])
    dy, d_gain, d_shift = norm_backward(d_dec, unit, rstd, vec_ref[0:1])
    xb = jnp.concatenate([x_ref[...].astype(F32), jnp.zeros((FR - Q, D), F32)], 0).astype(BF)
    _, d_w = attend_backward(
        dy, xb, q_ref[...], k_ref[...], v_ref[...], m_ref[...], p_ref, w_ref[0], w_ref[1], w_ref[2], w_ref[3]
    )
    d_wq = dot_tn(dec_ref[...].astype(BF), grad)
    front = jnp.concatenate([d_gain, d_shift, jnp.zeros((8, D), F32), jnp.sum(dy, 0, keepdims=True), jnp.zeros((13, D), F32)], 0)
    d_vec = dpost_ref[...] + front
    d_w = [w.astype(BF) for w in d_w]
    d_wq = d_wq.astype(BF)
    d_vec = d_vec.astype(BF)
    first, second = own, 1 - own
    for shard in range(SHARDS):
        n = me ^ shard
        at = slice(shard * RS, (shard + 1) * RS)
        for m in range(4):
            all_ref[first, n, m * RS : (m + 1) * RS] = d_w[m][at]
        all_ref[second, n, :RS] = jnp.zeros((RS, D), BF)
        all_ref[second, n, RS : 2 * RS] = d_wq[at, :D]
        right = d_wq[at, D:]
        all_ref[second, n, 2 * RS : 2 * RS + RS // 2] = jnp.concatenate([right[: RS // 2], right[RS // 2 :]], 1)
        all_ref[second, n, 2 * RS + RS // 2 : 128] = jnp.concatenate([d_vec, jnp.zeros((24, D), BF)], 0)
    mine_ref[...] = all_ref[0]
    send_ref[...] = all_ref[1]


def front_backward(*args):
    half = jax.ShapeDtypeStruct((SHARDS, 128, D), BF)
    return pl.pallas_call(
        front_back_kernel,
        in_specs=[SM] + [VM] * 16,
        out_specs=[VM, VM],
        out_shape=[half, half],
        scratch_shapes=[pltpu.VMEM((2, SHARDS, 128, D), BF)],
        compiler_params=params(),
        cost_estimate=cost(2_000_000_000, 5_000_000),
        name="front_backward",
    )(*args)


def smooth_max(a, b):
    return 0.5 * (a + b + jnp.sqrt((a - b) * (a - b) + SMOOTHING))


def smooth_min(a, b):
    return 0.5 * (a + b - jnp.sqrt((a - b) * (a - b) + SMOOTHING))


def box_cost(p, t):
    distance = sum(jnp.sqrt((a - b) * (a - b) + 0.01) for a, b in zip(p, t))
    inter = hull = None
    for axis in range(2):
        p_low, p_up = p[axis] - 0.5 * p[axis + 2], p[axis] + 0.5 * p[axis + 2]
        t_low, t_up = t[axis] - 0.5 * t[axis + 2], t[axis] + 0.5 * t[axis + 2]
        over = smooth_max(smooth_min(p_up, t_up) - smooth_max(p_low, t_low), 0.0)
        enclose = smooth_max(p_up, t_up) - smooth_min(p_low, t_low)
        inter, hull = (over, enclose) if inter is None else (inter * over, hull * enclose)
    union = p[2] * p[3] + t[2] * t[3] - inter
    general = inter / union - (hull - union) / hull
    return 5.0 * distance + 2.0 * (1.0 - general)


LOSS_UNITS = [16.0 ** (3 - n) for n in range(8)]
LATE = 23 * RS // 2


def unpack_late(me, own, mine, other, ws_ref, fi_ref, fo_ref):
    def take(halves):
        for n in range(SHARDS):
            shard = me ^ order(LATE_BITS)[n]
            at = pl.ds(pl.multiple_of(shard * RS, RS), RS)

            def rows(block):
                parts = []
                for p in (block * RS, block * RS + RS // 2):
                    parts.append(halves[p // LATE][n // 4][n % 4, p % LATE : p % LATE + RS // 2])
                return jnp.concatenate(parts, 0)

            for m in range(7):
                ws_ref[m, at] = rows(m)
            for i in range(2):
                for c in range(4):
                    fi_ref[i, at, c * D : (c + 1) * D] = rows(7 + 4 * i + c)
                    down = pl.ds(pl.multiple_of((4 * shard + c) * RS, RS), RS)
                    fo_ref[i, down] = rows(15 + 4 * i + c)

    @pl.when(own == 0)
    def _():
        take((mine, other))

    @pl.when(own == 1)
    def _():
        take((other, mine))


def post_kernel(
    ids_ref, match_ref, count_ref, s_ref, add_ref, dec_ref, tgt_ref, late_a, late_b, late_c, late_d, vec_ref,
    ds_ref, dres_ref, mine_ref, send_ref, dvec_ref,
    ws_ref, fi_ref, fo_ref, all_ref, p_ref, box_ref, pick_ref,
):
    own = ids_ref[1]
    f = own
    me = ids_ref[2]
    unpack_late(me, own, (late_a, late_b), (late_c, late_d), ws_ref, fi_ref, fo_ref)
    dvec_ref[...] = jnp.zeros_like(dvec_ref)
    kept, given = own, 1 - own

    def put_square(m, grad):
        grad = grad.astype(BF)
        for n in range(SHARDS):
            all_ref[kept, me ^ n, m * RS : (m + 1) * RS] = grad[n * RS : (n + 1) * RS]

    def put_in(i, grad):
        grad = grad.astype(BF)
        for n in range(SHARDS):
            for c in range(4):
                piece = grad[n * RS : (n + 1) * RS, c * D : (c + 1) * D]
                if i == 0:
                    all_ref[kept, me ^ n, (7 + c) * RS : (8 + c) * RS] = piece
                else:
                    all_ref[given, me ^ n, c * RS : (c + 1) * RS] = piece

    def put_out(i, grad):
        grad = grad.astype(BF)
        for n in range(SHARDS):
            all_ref[given, me ^ n, (4 + 4 * i) * RS : (8 + 4 * i) * RS] = grad[n * 4 * RS : (n + 1) * 4 * RS]

    vec = lambda row: vec_ref[row : row + 1]
    total = lambda value: jnp.sum(value, 0, keepdims=True)

    def add_vec(row, value):
        dvec_ref[row : row + 1] += value

    sb = (s_ref[...].astype(F32) + add_ref[...].astype(F32)).astype(BF)
    first, unit2, rstd2 = norm_forward(dec_ref[...] + dot(sb, ws_ref[0]) + vec(11), vec(2), vec(3))
    firstb = first.astype(BF)
    hid1, slope1 = gelu_pair(dot(firstb, fi_ref[0]))
    hid1 = hid1.astype(BF)
    second, unit3, rstd3 = norm_forward(first + dot(hid1, fo_ref[0]) + vec(12), vec(4), vec(5))
    y4, secondb, q, k, v, mixed = attend_forward(second, ws_ref[1], ws_ref[2], ws_ref[3], ws_ref[4], vec(13), p_ref)
    third, unit4, rstd4 = norm_forward(y4, vec(6), vec(7))
    thirdb = third.astype(BF)
    hid2, slope2 = gelu_pair(dot(thirdb, fi_ref[1]))
    hid2 = hid2.astype(BF)
    fourth, unit5, rstd5 = norm_forward(third + dot(hid2, fo_ref[1]) + vec(14), vec(8), vec(9))
    fourthb = fourth.astype(BF)
    z1, slope_z1 = gelu_pair(dot(fourthb, ws_ref[5]) + vec(15))
    z1 = z1.astype(BF)
    z2, slope_z2 = gelu_pair(dot(z1, ws_ref[6]) + vec(16))
    z2 = z2.astype(BF)
    w3 = jnp.concatenate([vec_ref[17:21], jnp.zeros((124, D), F32)], 0).astype(BF)
    boxes = jax.nn.sigmoid(dot_nt(z2, w3))
    box_ref[...] = boxes
    slots = tgt_ref.shape[1]
    for o in range(slots):
        pick_ref[o : o + 1, :] = box_ref[pl.ds(match_ref[f, o], 1), :]
    picked = pick_ref[...]
    pred = [picked[:, c : c + 1] for c in range(4)]
    target = [tgt_ref[own, :, c : c + 1] for c in range(4)]
    valid = (lax.broadcasted_iota(jnp.int32, (slots, 1), 0) < count_ref[f]).astype(F32)
    price, pull = jax.vjp(lambda *p: box_cost(p, target), *pred)
    loss = jnp.sum(valid * price, 0, keepdims=True)
    count = jnp.sum(vec_ref[21:22], -1, keepdims=True) / RS
    d_pred = pull(valid / count)
    lane = lane_iota(slots)
    rows = jnp.zeros((slots, 128), F32)
    for c in range(4):
        rows = jnp.where(lane == c, d_pred[c], rows)
    pick_ref[...] = rows
    box_ref[...] = jnp.zeros((FR, 128), F32)
    for o in range(slots):
        box_ref[pl.ds(match_ref[f, o], 1), :] = pick_ref[o : o + 1, :]
    d_logit = (box_ref[...] * boxes * (1.0 - boxes)).astype(BF)
    dvec_ref[17:21] += dot_tn(d_logit, z2)[0:4]
    du = dot(d_logit, w3) * slope_z2
    add_vec(16, total(du))
    du = du.astype(BF)
    put_square(6, dot_tn(z1, du))
    du = dot_nt(du, ws_ref[6]) * slope_z1
    add_vec(15, total(du))
    du = du.astype(BF)
    put_square(5, dot_tn(fourthb, du))
    grad = dot_nt(du, ws_ref[5])

    def ffn_back(grad, unit, rstd, i, row, bias, hid, slope, inputb):
        dy, d_gain, d_shift = norm_backward(grad, unit, rstd, vec(row))
        add_vec(row, d_gain)
        add_vec(row + 1, d_shift)
        add_vec(bias, total(dy))
        dyb = dy.astype(BF)
        put_out(i, dot_tn(hid, dyb))
        du = (dot_nt(dyb, fo_ref[i]) * slope).astype(BF)
        put_in(i, dot_tn(inputb, du))
        return dy + dot_nt(du, fi_ref[i])

    grad = ffn_back(grad, unit5, rstd5, 1, 8, 14, hid2, slope2, thirdb)
    dy, d_gain, d_shift = norm_backward(grad, unit4, rstd4, vec(6))
    add_vec(6, d_gain)
    add_vec(7, d_shift)
    add_vec(13, total(dy))
    grad, d_w = attend_backward(dy, secondb, q, k, v, mixed, p_ref, ws_ref[1], ws_ref[2], ws_ref[3], ws_ref[4])
    for i in range(4):
        put_square(1 + i, d_w[i])
    grad = ffn_back(grad, unit3, rstd3, 0, 4, 12, hid1, slope1, firstb)
    dy, d_gain, d_shift = norm_backward(grad, unit2, rstd2, vec(2))
    add_vec(2, d_gain)
    add_vec(3, d_shift)
    add_vec(11, total(dy))
    dres_ref[...] = dy
    dyb = dy.astype(BF)
    put_square(0, dot_tn(sb, dyb))
    ds_ref[...] = dot_nt(dyb, ws_ref[0]).astype(BF)
    row = lax.broadcasted_iota(jnp.int32, (RS, D), 0)
    rows, above = jnp.zeros((RS, D), F32), jnp.zeros((1, 1), F32)
    for n, unit in enumerate(LOSS_UNITS):
        whole = jnp.floor(loss * (1.0 / unit))
        rows = jnp.where(row == n, whole - 16.0 * above, rows)
        above = whole
    rows = rows.astype(BF)
    for n in range(SHARDS):
        all_ref[kept, me ^ n, 11 * RS : 12 * RS] = rows
    mine_ref[...] = all_ref[0]
    send_ref[...] = all_ref[1]


def post_step(ids, match, count, half, add, dec, target, late, vec):
    half_rows = jax.ShapeDtypeStruct((SHARDS, 12 * RS, D), BF)
    return pl.pallas_call(
        post_kernel,
        in_specs=[SM, SM, SM] + [VM] * 9,
        out_specs=[VM] * 5,
        out_shape=[frame_rows(BF), frame_rows(F32), half_rows, half_rows, jax.ShapeDtypeStruct((24, D), F32)],
        scratch_shapes=[
            pltpu.VMEM((7, D, D), BF),
            pltpu.VMEM((2, D, 4 * D), BF),
            pltpu.VMEM((2, 4 * D, D), BF),
            pltpu.VMEM((2, SHARDS, 12 * RS, D), BF),
            pltpu.VMEM((H, FR, FR), BF),
            pltpu.VMEM((FR, 128), F32),
            pltpu.VMEM((target.shape[1], 128), F32),
        ],
        compiler_params=params(DENSE_LIMIT),
        cost_estimate=cost(8_000_000_000, 10_000_000),
        name="post_step",
    )(ids, match, count, half, add, dec, target, *late, vec)


LEARNING_RATE = 2.0
MOMENTUM = 0.5
AVERAGING = 0.5


def update(master, gradient, moment, average):
    moment_new = MOMENTUM * moment + gradient
    master_new = master - LEARNING_RATE * (gradient + MOMENTUM * moment_new)
    average_new = AVERAGING * average + (1.0 - AVERAGING) * master_new
    return (master_new, master_new.astype(BF), moment_new, average_new)


def apply_kernel(ids_ref, last_mine, last_other, late_mine, late_other, *refs):
    own, me = ids_ref[1], ids_ref[2]
    masters, moments, averages, loss_ref, outs = refs[:5], refs[5:10], refs[10:15], refs[15], refs[16:]

    def halves(mine, other):
        mine, other = mine[...], other[...]
        return jnp.where(own == 0, mine, other), jnp.where(own == 0, other, mine)

    last, late = halves(last_mine, last_other), halves(late_mine, late_other)

    def step(which, index, grad):
        new = update(masters[which][index], grad, moments[which][index], averages[which][index])
        for out, value in zip(outs[4 * which : 4 * which + 4], new):
            out[index] = value

    def block(rows, n, count=1):
        return rows[n * RS : (n + count) * RS]

    step(0, (slice(None), slice(0, D)), block(last[1], 1))
    right = last[1][2 * RS : 2 * RS + RS // 2]
    step(0, (slice(0, RS // 2), slice(D, D + 128)), right[:, :128])
    step(0, (slice(RS // 2, RS), slice(D, D + 128)), right[:, 128:])
    for m in range(12):
        step(1, (m,), block(last[0], m) if m < 4 else block(last[1], 0) if m == 4 else block(late[0], m - 5))
    for i in range(2):
        for c in range(4):
            step(2, (i, slice(None), slice(c * D, (c + 1) * D)), block(late[1], c) if i else block(late[0], 7 + c))
        step(3, (i,), block(late[1], 4 + 4 * i, 4))
    vec = last[1][2 * RS + RS // 2 : 2 * RS + RS // 2 + 24]
    vec = jnp.where(me >= 4, vec[:, 128:], vec[:, :128])
    vec = pltpu.roll(vec, (4 - me % 4) % 4 * RS, 1)
    step(4, (slice(None), slice(None)), vec[:21, :RS])
    loss_ref[...] = sum(late[0][11 * RS + n : 11 * RS + n + 1, 0:1] * unit for n, unit in enumerate(LOSS_UNITS))


def apply_updates(ids, grads, masters, moments, averages):
    shapes = [jax.ShapeDtypeStruct((1, 1), F32)]
    for master in masters:
        full = jax.ShapeDtypeStruct(master.shape, F32)
        shapes += [full, jax.ShapeDtypeStruct(master.shape, BF), full, full]
    loss, *outs = pl.pallas_call(
        apply_kernel,
        in_specs=[SM] + [VM] * 19,
        out_specs=[VM] * 21,
        out_shape=shapes,
        compiler_params=params(24 * 1024 * 1024),
        cost_estimate=cost(3_000_000, 8_000_000),
        name="apply_updates",
    )(ids, *grads, *masters, *moments, *averages)
    return loss.reshape(()), outs


def pairs(size, bit):
    return [(i, i ^ bit) for i in range(size)]


def swap_core(value):
    return lax.ppermute(value, "level", pairs(4, 1))


def swap_chip(value):
    return lax.ppermute(value, "level", pairs(4, 2))


def pick(pair, index):
    return lax.dynamic_index_in_dim(pair, index, 0, keepdims=False)


def in_order(mine, other, index):
    return jnp.where(index == 0, mine, other), jnp.where(index == 0, other, mine)


def early_rows(square, query, vec):
    right = jnp.concatenate([query[: RS // 2, D:], query[RS // 2 :, D:]], 1)
    second = jnp.concatenate([square[4], query[:, :D], right, vec, jnp.zeros((24, D), vec.dtype)], 0)
    return jnp.stack([square[:4].reshape(4 * RS, D), second])


def late_rows(square, ffn_in, ffn_out):
    return jnp.concatenate(
        [
            square.reshape(7 * RS, D),
            ffn_in.reshape(2, RS, 4, D).transpose(0, 2, 1, 3).reshape(8 * RS, D),
            ffn_out.reshape(8 * RS, D),
        ],
        0,
    )


def gather_weights(dp, own, rows, w_query, w_square, w_ffn_in, w_ffn_out, vectors, count):
    rs = D // dp
    shard = lax.axis_index("dp")
    here = jnp.arange(D, dtype=jnp.int32)[None, :] // rs == shard
    vec = jnp.where(here, jnp.tile(jnp.pad(vectors, ((0, 3), (0, 0))), (1, dp)), 0.0)
    vec = jnp.where(here & (jnp.arange(24)[:, None] == 21), count, vec)
    if dp == SHARDS:
        early = pick(early_rows(w_square[:5], w_query, vec).astype(BF), own)[None]
        first = lax.ppermute(early, "dp", pairs(dp, EARLY_BITS[0]))
        early, first, *late = lax.optimization_barrier((early, first, w_square[5:], w_ffn_in, w_ffn_out))
        late = pick(late_rows(*(w.astype(BF) for w in late)).reshape(2, -1, D), own)[None]
        early, late, rows = lax.optimization_barrier((jnp.concatenate([early, first], 0), late, rows))
        second = lax.ppermute(early, "dp", pairs(dp, EARLY_BITS[1]))
        late_first = lax.ppermute(late, "dp", pairs(dp, LATE_BITS[0]))
        early = jnp.concatenate([early, second], 0)
        late = jnp.concatenate([late, late_first], 0)
        early, late = lax.optimization_barrier((early, late))
        third = lax.ppermute(early, "dp", pairs(dp, EARLY_BITS[2]))
        late = (late, lax.ppermute(late, "dp", pairs(dp, LATE_BITS[1])))
        early = jnp.concatenate([early, third], 0)
        return rows, early, swap_core(early), late

    def whole(weight, dim):
        return lax.all_gather(weight.astype(BF), "dp", axis=dim, tiled=True)

    square, query = whole(w_square, 1), whole(w_query, 0)
    ffn_in, ffn_out = whole(w_ffn_in, 1), whole(w_ffn_out, 1)
    vec = lax.psum(vec, "dp")
    early, late = [], []
    for n in order(EARLY_BITS):
        at = slice(n * RS, (n + 1) * RS)
        columns = jnp.where(jnp.arange(D)[None, :] // RS == n, vec, 0.0).astype(BF)
        early.append(early_rows(square[:5, at], query[at], columns))
    for n in order(LATE_BITS):
        at = slice(n * RS, (n + 1) * RS)
        late.append(late_rows(square[5:, at], ffn_in[:, at], ffn_out[:, 4 * n * RS : 4 * (n + 1) * RS]))
    early = jnp.stack(early, 1)
    late = pick(jnp.stack(late).reshape(SHARDS, 2, -1, D).transpose(1, 0, 2, 3), own).reshape(2, 4, -1, D)
    return rows, pick(early, own), pick(early, 1 - own), late


def halve(value):
    value = value.reshape(-1, 2, *value.shape[1:])
    return value[:, 0], value[:, 1].astype(BF)


def send(value, bit):
    return lax.ppermute(value, "dp", pairs(SHARDS, bit)).astype(F32)


def after(value, event):
    return lax.optimization_barrier((value, event))[0]


def shards(
    queries, memory, frame_size, sample_pick, target_box, match, obj_count,
    w_query, w_square, w_ffn_in, w_ffn_out, vectors,
    m_query, m_square, m_ffn_in, m_ffn_out, m_vectors,
    a_query, a_square, a_ffn_in, a_ffn_out, a_vectors,
):
    dp = lax.axis_size("dp")
    rs = D // dp
    shard = lax.axis_index("dp")
    level = lax.axis_index("level")
    own = level % 2
    me = shard if dp == SHARDS else 0
    ids = jnp.stack([level, own, me, 0]).astype(jnp.int32)
    rows = pick_rows(frame_size, ids, sample_pick[:, 0, :].T)
    rows, mine, other, late = gather_weights(
        dp, own, rows, w_query, w_square, w_ffn_in, w_ffn_out, vectors, jnp.sum(obj_count).astype(F32)
    )
    memory_t = memory.transpose(1, 2, 0, 3)
    x = pick(queries.reshape(2, Q, D), own)
    w4, wq, s4, vec, total, dec, y, q, k, v, mixed, p, fa, fa_send, att = front_forward(ids, x, mine, other)
    fa_other = swap_core(fa_send)
    if dp == SHARDS:
        late = jnp.concatenate([late[0], after(late[1], att)], 0)
        s4 = after(s4, late)
        late = (late, lax.ppermute(late, "dp", pairs(dp, LATE_BITS[2])))
    gathered, part, part_send = sample_forward(rows, frame_size, ids, memory_t, s4, fa, fa_other)
    part_other = swap_core(part_send)
    half = (part.astype(F32) + part_other.astype(F32)).astype(BF)
    half_other = swap_chip(half)
    late_end = after(late[1], part_other)
    late = (late[0], late_end, swap_core(late[0]), swap_core(late_end))
    ds, dres, late_mine, late_send, dvec = post_step(
        ids, match, obj_count, half, half_other, dec, target_box, late, vec
    )
    ds_other = swap_core(ds)
    late_sent = swap_core(after(late_send, ds_other))
    gp, gp_send = coef_backward(ids, gathered, ds, ds_other, fa, fa_other)
    near = jnp.stack([gp, swap_core(gp_send)])
    far = swap_chip(near)
    late_sum = late_mine.astype(F32) + late_sent.astype(F32)
    late_kept, late_out = halve(late_sum)
    near, late_out, ds_other = lax.optimization_barrier((near, late_out, ds_other))
    if dp == SHARDS:
        late_in = send(late_out, 1)
    d_s4 = sample_backward(rows, frame_size, ids, memory_t, ds, ds_other, fa, fa_other)
    d_s4_other = swap_chip(d_s4)
    if dp == SHARDS:
        late_kept, late_out = halve(late_kept + after(late_in, d_s4))
        near, late_out = lax.optimization_barrier((near, late_out))
        late_in = send(late_out, 2)
    last_mine, last_send = front_backward(
        ids, near, far, att, dres, x, dec, y, q, k, v, mixed, p, w4, wq, vec, dvec
    )
    d_s4 = (d_s4.astype(F32) + d_s4_other.astype(F32)).astype(BF)
    d_s4 = d_s4.astype(F32) + swap_core(d_s4).astype(F32)
    last_sent = swap_core(last_send)
    d_s4 = jnp.pad(jnp.where(own == 1, d_s4, 0.0), ((0, 0), (0, 128 - RS), (0, 0)))
    last = last_mine.astype(F32) + last_sent.astype(F32) + d_s4
    if dp == SHARDS:
        late_kept, late_out = halve(late_kept + after(late_in, last_sent))
        last, late_out = lax.optimization_barrier((last, late_out))
        late_in = send(late_out, 4)
        for bit in (1, 2, 4):
            last_kept, last_out = halve(last)
            last = last_kept + send(last_out, bit)
        late_sum = (late_kept + after(late_in, last))[0]
        last = last[0]
    masters = (w_query, w_square, w_ffn_in, w_ffn_out, vectors)
    moments = (m_query, m_square, m_ffn_in, m_ffn_out, m_vectors)
    averages = (a_query, a_square, a_ffn_in, a_ffn_out, a_vectors)
    last_other, late_other = swap_core(last), swap_core(late_sum)
    if dp == SHARDS:
        loss, outs = apply_updates(ids, (last, last_other, late_sum, late_other), masters, moments, averages)
    else:
        last, late = in_order(last, last_other, own), in_order(late_sum, late_other, own)
        loss = lax.psum(late[0][0, 11 * RS : 11 * RS + 8, 0], "dp")

        def square(rows):
            return rows.reshape(SHARDS, -1, RS, D).transpose(1, 0, 2, 3).reshape(-1, D, D)

        right = last[1][:, 2 * RS : 2 * RS + RS // 2].reshape(SHARDS, RS // 2, 2, 128).transpose(0, 2, 1, 3)
        g_query = jnp.concatenate([square(last[1][:, RS : 2 * RS])[0], right.reshape(D, 128)], 1)
        g_vec = last[1][0, 2 * RS + RS // 2 : 2 * RS + RS // 2 + 21]
        g_square = jnp.concatenate([square(last[0]), square(last[1][:, :RS]), square(late[0][:, : 7 * RS])], 0)
        g_in = [x.reshape(SHARDS, 4, RS, D).transpose(0, 2, 1, 3) for x in (late[0][:, 7 * RS : 11 * RS], late[1][:, : 4 * RS])]
        g_in = jnp.concatenate([x.reshape(1, D, 4 * D) for x in g_in], 0)
        g_out = late[1][:, 4 * RS :].reshape(SHARDS, 2, 4 * RS, D).transpose(1, 0, 2, 3).reshape(2, 4 * D, D)

        def scatter(grad, dim):
            return lax.psum_scatter(grad, "dp", scatter_dimension=dim, tiled=True)

        g_query, g_square, g_vec = scatter(g_query, 0), scatter(g_square, 1), scatter(g_vec, 1)
        g_in, g_out = scatter(g_in, 1), scatter(g_out, 1)
        grads = (g_query, g_square, g_in, g_out, g_vec)
        outs = [out for group in zip(masters, grads, moments, averages) for out in update(*group)]
        loss = jnp.sum(loss * jnp.array(LOSS_UNITS, F32))
    return (loss, total.reshape(()), *outs)


def solution(mesh):
    rows, mid, low = P("dp", None), P(None, "dp", None), P(None, "dp")
    five = (rows, mid, mid, mid, low)
    return jax.shard_map(
        shards,
        mesh=mesh,
        in_specs=(
            rows,
            P("dp", "level", None, None),
            rows,
            P("dp", "level", None),
            P("dp", None, None),
            rows,
            P("dp"),
        )
        + five * 3,
        out_specs=(P(), P()) + tuple(spec for spec in five for _ in range(4)),
        check_vma=False,
    )
```

```python
import jax
import jax.numpy as jnp
from jax import lax
from jax.experimental import pallas as pl
from jax.experimental.pallas import tpu as pltpu
from jax.sharding import PartitionSpec as P

D = 256
H = 8
P_SIZE = 4
Q = 300
MCAP = 16700
FR = 304
R = 2 * FR
NB = R // 4
PAD = 8
STRIDE = 168
ROWS = 100
TABLE = PAD + (ROWS + 1) * STRIDE + PAD
STAGE = 19
COPIES = 4
SHARDS = 8
RS = D // SHARDS
EARLY_BITS = (4, 2, 1)
LATE_BITS = (1, 2, 4)
EARLY_SUM_BITS = (1, 2, 4)
LATE_SUM_BITS = (1, 2, 4)


def place(shard, bits):
    return sum((shard >> (bit // 2) & 1) << 2 - i for i, bit in enumerate(bits))
BF = jnp.bfloat16
F32 = jnp.float32
VMEM_LIMIT = 62 * 1024 * 1024


def lane_iota(rows):
    return lax.broadcasted_iota(jnp.int32, (rows, 128), 1)


def dot(a, b):
    return jnp.dot(a, b, preferred_element_type=F32)


def dot_nt(a, b):
    return lax.dot_general(a, b, (((1,), (1,)), ((), ())), preferred_element_type=F32)


def dot_tn(a, b):
    return lax.dot_general(a, b, (((0,), (0,)), ((), ())), preferred_element_type=F32)


def expand_matrix(point, dy):
    row = lax.broadcasted_iota(jnp.int32, (128, 256), 0)
    col = lax.broadcasted_iota(jnp.int32, (128, 256), 1) // 32
    return (row == dy * 32 + col * 4 + point).astype(F32).astype(BF)


def fold_matrix(point):
    row = lax.broadcasted_iota(jnp.int32, (256, 128), 0) // 32
    col = lax.broadcasted_iota(jnp.int32, (256, 128), 1)
    return (col == row * 4 + point).astype(F32).astype(BF)


def join_frames(own, mine_ref, other_ref, scr):
    scr[own] = mine_ref[...]
    scr[1 - own] = other_ref[...]
    return scr[...].reshape(R, scr.shape[-1])


def place_coefs(fa, scr):
    lane = lane_iota(R)
    low = lane < 32
    r32, r64, r96 = pltpu.roll(fa, 32, 1), pltpu.roll(fa, 64, 1), pltpu.roll(fa, 96, 1)
    fx = jnp.where(low, fa, r32)
    cy = jnp.where(low, 1.0 - r96, fa)
    att = jnp.where(low, r64, r96)
    base = jnp.where(lane < 64, att * cy, 0.0)
    for dx in range(2):
        coef = base * (fx if dx else 1.0 - fx)
        for k in range(4):
            scr[pl.ds(2 * k + dx, NB, 8), :] = coef[k * NB : (k + 1) * NB]


def fill_weights(scr, wexp):
    packed = scr[...].astype(BF)
    for point in range(4):
        for dy in range(2):
            wexp[point * 2 + dy] = dot(packed, expand_matrix(point, dy)).astype(wexp.dtype)


def row_masks():
    lane = lane_iota(8) // 32
    sub = lax.broadcasted_iota(jnp.int32, (8, 128), 0)
    heads = [lane == h for h in range(4)]
    rows = [sub // 2 == k for k in range(4)]
    return heads, rows


def pick_copies(idx_ref, picks, sem):
    return [pltpu.make_async_copy(idx_ref.at[c % 4, c // 4], picks[c], sem) for c in range(128)]


class Chunks:
    def __init__(self, mem_ref, buf, stage, sems, size_ref, ids_ref):
        self.mem_ref, self.buf, self.stage, self.sems = mem_ref, buf, stage, sems
        self.slots, self.cells = buf.shape[:2]
        level = ids_ref[0]
        self.high, self.wide = (
            [(size_ref[f, axis] + (1 << level) - 1) >> level for f in range(2)] for axis in range(2)
        )
        used = jnp.maximum(self.high[0] * self.wide[0], self.high[1] * self.wide[1])
        self.count = lax.div(used + self.cells - 1, self.cells)
        self.inner = slice(2 * STRIDE, 2 * STRIDE + 2 * self.cells)
        self.whole = -(-MCAP // self.cells)
        self.again = self.whole * self.cells - MCAP

    def base(self, j):
        return jnp.minimum(j * self.cells, MCAP - self.cells)

    def grid_rows(self, cell, f):
        return lax.div(jnp.minimum(cell, MCAP), self.wide[f])

    def copies(self, j, slot):
        size = self.cells // COPIES
        return [
            pltpu.make_async_copy(
                self.mem_ref.at[0, pl.ds(self.base(j) + c * size, size)],
                self.buf.at[slot, pl.ds(c * size, size)],
                self.sems.at[slot, c],
            )
            for c in range(COPIES)
        ]

    def start(self, j):
        @pl.when(j < self.count)
        def _():
            for copy in self.copies(j, lax.rem(j, self.slots)):
                copy.start()

    def start_all(self):
        for j in range(self.slots - 1):
            self.start(jnp.int32(j))

    def staged(self, i, f, j):
        return pl.ds(2 * (i * self.wide[f] - self.base(j) + STRIDE) + f, STRIDE, 2)

    def run(self, work):
        def body(j, carry):
            slot = lax.rem(j, self.slots)
            self.start(j + self.slots - 1)
            for copy in self.copies(j, slot):
                copy.wait()
            work(j, self.buf[slot].reshape(2 * self.cells, D))
            return carry

        lax.fori_loop(0, self.count, body, 0)


def grid_row(i):
    return pl.ds(pl.multiple_of(i * STRIDE, 8) + PAD, STRIDE)


def pick_kernel(size_ref, ids_ref, pick_ref, out_ref):
    level = ids_ref[0]
    frame = lax.broadcasted_iota(jnp.int32, (1, 2 * Q), 1) >= Q

    def of_frame(column):
        first, second = ((size_ref[f, column] + (1 << level) - 1) >> level for f in range(2))
        return jnp.where(frame, second, first).astype(F32)

    def rest(values, most):
        m = jnp.maximum(most - 1.0, 1.0)
        left = values - jnp.floor(values * (1.0 / m)) * m
        left = jnp.where(left < 0.0, left + m, left)
        return jnp.where(left >= m, left - m, left)

    picks = pick_ref[...].astype(F32)
    cell = rest(picks[:32], of_frame(0)) * STRIDE + rest(picks[32:], of_frame(1))
    row = cell.astype(jnp.int32)
    for k in range(4):
        first = (k // 2) * Q + (k % 2) * NB
        width = NB if k % 2 == 0 else Q - NB
        out_ref[k, :, :width] = row[:, first : first + width]
        if width < NB:
            out_ref[k, :, width:] = jnp.zeros((32, NB - width), jnp.int32)


def pick_rows(size, ids, picks):
    return pl.pallas_call(
        pick_kernel,
        in_specs=[SM, SM, VM],
        out_specs=VM,
        out_shape=jax.ShapeDtypeStruct((4, 32, NB), jnp.int32),
        name="pick_rows",
    )(size, ids, picks)


def forward_kernel(
    idx_ref, size_ref, ids_ref, mem_ref, s4_ref, mine_ref, other_ref,
    g_ref, out_ref, send_ref,
    buf, stage, tables, wexp, racc, cscr, fscr, gscr, gtmp, sems, isem, gsems, *picks,
):
    own = ids_ref[1]
    chunks = Chunks(mem_ref, buf, stage, sems, size_ref, ids_ref)
    chunks.start_all()
    for copy in pick_copies(idx_ref, picks, isem):
        copy.start()
    place_coefs(join_frames(own, mine_ref, other_ref, fscr), cscr)
    fill_weights(cscr, wexp)

    def fill(j, m):
        v = dot(m, s4_ref[...])
        for half in range(2):
            stage[half, chunks.inner, :] = v[:, half * 128 : half * 128 + 128]
        for f in range(2):
            first = chunks.grid_rows(j * chunks.cells, f)
            last = jnp.minimum(chunks.grid_rows((j + 1) * chunks.cells, f), chunks.high[f])

            def copy_row(i, carry):
                for half in range(2):
                    tables[f][half][grid_row(i), :] = stage[half, chunks.staged(i, f, j), :]
                return carry

            lax.fori_loop(first, last, copy_row, 0)
        for half in range(2):
            kept = pl.ds(2 * (chunks.base(j + 1) - chunks.base(j)), 2 * STRIDE)
            stage[half, : 2 * STRIDE, :] = stage[half, kept, :]

    chunks.run(fill)
    for copy in pick_copies(idx_ref, picks, isem):
        copy.wait()
    heads, rows = row_masks()

    def block(j):
        found = [None] * 16
        for half in range(2):
            for point in range(4):
                acc = None
                for h in range(4):
                    part = None
                    for k in range(4):
                        r = picks[((half * 4 + h) * 4 + point) * 4 + k][j] + (PAD - 2 * k)
                        table = tables[k // 2][half]
                        new = (table[pl.ds(r, 8), :], table[pl.ds(r + STRIDE, 8), :])
                        part = new if part is None else [jnp.where(rows[k], x, y) for x, y in zip(new, part)]
                    acc = part if acc is None else [jnp.where(heads[h], x, y) for x, y in zip(part, acc)]
                found[half * 8 + point * 2], found[half * 8 + point * 2 + 1] = acc
        return found

    def gather_block(j, carry):
        low = pl.ds(pl.multiple_of((j % 2) * 8, 8), 8)
        for n, found in enumerate(block(j)):
            gtmp[n, low, :] = found
        return carry

    def gather(i, carry):
        lax.fori_loop(2 * i, 2 * i + 2, gather_block, 0)
        at = pl.ds(pl.multiple_of(i * 16, 16), 16)
        for half in range(2):
            lanes = slice(half * 128, half * 128 + 128)
            total = None
            for pd in range(8):
                g = gtmp[half * 8 + pd]
                gscr[pd, at, lanes] = g.astype(BF)
                v = g * wexp[pd, at, lanes].astype(F32)
                total = v if total is None else total + v
            racc[half, at, :] = total
        return carry

    def keep(stage):
        at = pl.ds(pl.multiple_of(stage * STAGE * 16, 16), STAGE * 16)
        return pltpu.make_async_copy(gscr.at[:, at], g_ref.at[:, at], gsems.at[stage])

    def gather_stage(stage, carry):
        lax.fori_loop(stage * STAGE, (stage + 1) * STAGE, gather, 0)
        keep(stage).start()
        return carry

    lax.fori_loop(0, NB // 2 // STAGE, gather_stage, 0)
    for half in range(2):
        a = racc.at[half]
        lanes = slice(half * 128, half * 128 + 128)
        for k in range(2):
            at = slice(k * NB, (k + 1) * NB)
            first, second = (
                (a[pl.ds(2 * n, NB, 8), :] + a[pl.ds(2 * n + 1, NB, 8), :]).astype(BF) for n in (k, k + 2)
            )
            out_ref[at, lanes] = jnp.where(own == 0, first, second)
            send_ref[at, lanes] = jnp.where(own == 0, second, first)
    for stage in range(NB // 2 // STAGE):
        keep(stage).wait()


ANY = pl.BlockSpec(memory_space=pl.ANY)
SM = pl.BlockSpec(memory_space=pltpu.SMEM)
VM = pl.BlockSpec(memory_space=pltpu.VMEM)


def sampling_scratch(slots, cells):
    return [
        pltpu.VMEM((slots, cells, 2, D), BF),
        pltpu.VMEM((2, 2 * (cells + 2 * STRIDE), 128), F32),
        [[pltpu.VMEM((TABLE, 128), F32)] * 2] * 2,
        pltpu.VMEM((8, 2 * R, D), BF),
        pltpu.VMEM((2, 2 * R, 128), F32),
        pltpu.VMEM((2 * R, 128), F32),
        pltpu.VMEM((2, FR, 128), F32),
    ]


def sampling_semaphores(slots):
    return [pltpu.SemaphoreType.DMA((slots, COPIES)), pltpu.SemaphoreType.DMA(())]


def pick_scratch():
    return [pltpu.SMEM((NB,), jnp.int32)] * 128


def params(limit=VMEM_LIMIT):
    return pltpu.CompilerParams(vmem_limit_bytes=limit)


def cost(flops, moved):
    return pl.CostEstimate(flops=flops, bytes_accessed=moved, transcendentals=0)


def sample_forward(idx, size, ids, memory_t, s4, fa_mine, fa_other):
    frame = jax.ShapeDtypeStruct((FR, D), BF)
    return pl.pallas_call(
        forward_kernel,
        in_specs=[ANY, SM, SM, ANY, VM, VM, VM],
        out_specs=[ANY, VM, VM],
        out_shape=[jax.ShapeDtypeStruct((8, 2 * R, D), BF), frame, frame],
        scratch_shapes=sampling_scratch(4, 1680)
        + [pltpu.VMEM((8, 2 * R, D), BF), pltpu.VMEM((16, 16, 128), F32)]
        + sampling_semaphores(4)
        + [pltpu.SemaphoreType.DMA((NB // 2 // STAGE,))]
        + pick_scratch(),
        compiler_params=params(),
        cost_estimate=cost(30_000_000_000, 60_000_000),
        name="sample_forward",
    )(idx, size, ids, memory_t, s4, fa_mine, fa_other)


def place_grads(ds, g2):
    ds = ds.astype(F32)
    for half in range(2):
        for k in range(4):
            piece = ds[k * NB : (k + 1) * NB, half * 128 : half * 128 + 128]
            for dx in range(2):
                g2[half, pl.ds(2 * k + dx, NB, 8), :] = piece


def coef_kernel(
    ids_ref, g_ref, ds_mine, ds_other, fa_mine, fa_other, out_ref, send_ref, g2, scr, dscr, fscr
):
    own = ids_ref[1]
    place_grads(join_frames(own, ds_mine, ds_other, dscr), g2)
    fa_all = join_frames(own, fa_mine, fa_other, fscr)
    fold = [fold_matrix(point) for point in range(4)]
    for dy in range(2):
        total = None
        for point in range(4):
            for half in range(2):
                lanes = slice(half * 128, half * 128 + 128)
                v = (g_ref[point * 2 + dy, :, lanes].astype(F32) * g2[half]).astype(BF)
                v = dot(v, fold[point][half * 128 : half * 128 + 128])
                total = v if total is None else total + v
        scr[dy] = total
    lane = lane_iota(NB)
    results = []
    for k in range(4):
        at = slice(k * NB, (k + 1) * NB)
        g = [[scr[dy, pl.ds(2 * k + dx, NB, 8), :] for dx in range(2)] for dy in range(2)]
        fa = fa_all[at]
        fx, fy, att = fa, pltpu.roll(fa, 96, 1), pltpu.roll(fa, 64, 1)
        top = (1.0 - fx) * g[0][0] + fx * g[0][1]
        bottom = (1.0 - fx) * g[1][0] + fx * g[1][1]
        d_att = (1.0 - fy) * top + fy * bottom
        d_fy = att * (bottom - top)
        d_fx = att * ((1.0 - fy) * (g[0][1] - g[0][0]) + fy * (g[1][1] - g[1][0]))
        gx = d_fx * fx * (1.0 - fx)
        gy = pltpu.roll(d_fy * fy * (1.0 - fy), 32, 1)
        weighted = pltpu.roll(att * d_att, 64, 1)
        res = jnp.where(lane < 32, gx, jnp.where(lane < 64, gy, jnp.where(lane < 96, weighted, 0.0)))
        results.append(res.astype(BF))
    for k in range(2):
        at = slice(k * NB, (k + 1) * NB)
        out_ref[at] = jnp.where(own == 0, results[k], results[k + 2])
        send_ref[at] = jnp.where(own == 0, results[k + 2], results[k])


def coef_backward(ids, gathered, ds_mine, ds_other, fa_mine, fa_other):
    frame = jax.ShapeDtypeStruct((FR, 128), BF)
    return pl.pallas_call(
        coef_kernel,
        in_specs=[SM] + [VM] * 5,
        out_specs=[VM, VM],
        out_shape=[frame, frame],
        scratch_shapes=[
            pltpu.VMEM((2, 2 * R, 128), F32),
            pltpu.VMEM((2, 2 * R, 128), F32),
            pltpu.VMEM((2, FR, D), BF),
            pltpu.VMEM((2, FR, 128), F32),
        ],
        compiler_params=params(32 * 1024 * 1024),
        cost_estimate=cost(2_000_000_000, 10_000_000),
        name="coef_backward",
    )(ids, gathered, ds_mine, ds_other, fa_mine, fa_other)


def scatter_kernel(
    idx_ref, size_ref, ids_ref, mem_ref, ds_mine, ds_other, fa_mine, fa_other,
    out_ref,
    buf, stage, tables, wexp, g2, cscr, fscr, dscr, sems, isem, sum_ref, *picks,
):
    own = ids_ref[1]
    chunks = Chunks(mem_ref, buf, stage, sems, size_ref, ids_ref)
    for copy in pick_copies(idx_ref, picks, isem):
        copy.start()
    chunks.start_all()
    place_coefs(join_frames(own, fa_mine, fa_other, fscr), cscr)
    fill_weights(cscr, wexp)
    place_grads(join_frames(own, ds_mine, ds_other, dscr), g2)
    for pair in tables:
        for table in pair:
            table[:PAD, :] = jnp.zeros((PAD, 128), F32)
            table[TABLE - PAD :, :] = jnp.zeros((PAD, 128), F32)

    def clear(i, carry):
        for pair in tables:
            for table in pair:
                table[grid_row(i), :] = jnp.zeros((STRIDE, 128), F32)
        return carry

    lax.fori_loop(0, ROWS + 1, clear, 0)
    for copy in pick_copies(idx_ref, picks, isem):
        copy.wait()
    heads, rows = row_masks()

    def scatter(i, carry):
        at = pl.ds(pl.multiple_of(i * 16, 16), 16)
        for point in range(4):
            terms = [
                [wexp[point * 2 + dy, at, half * 128 : half * 128 + 128].astype(F32) * g2[half, at, :] for dy in range(2)]
                for half in range(2)
            ]
            for b in range(2):
                for low in range(2):
                    for half in range(2):
                        todo = []
                        for k in (low, low + 2):
                            for h in range(4):
                                r = picks[((half * 4 + h) * 4 + point) * 4 + k][2 * i + b] + (PAD - 2 * k)
                                table = tables[k // 2][half]
                                for dy in range(2):
                                    spot = pl.ds(r + dy * STRIDE, 8)
                                    value = table[spot, :] + terms[half][dy][8 * b : 8 * b + 8]
                                    todo.append((table, spot, value, heads[h] & rows[k]))
                        for table, spot, value, mask in todo:
                            pltpu.store(table.at[spot, :], value, mask=mask)
        return carry

    lax.fori_loop(0, NB // 2, scatter, 0)
    sum_ref[...] = jnp.zeros((D, D), F32)

    def reduce(j, m):
        for f in range(2):
            first = chunks.grid_rows(j * chunks.cells, f)
            last = chunks.grid_rows(jnp.minimum((j + 1) * chunks.cells, MCAP) - 1, f) + 1

            def copy_row(i, carry):
                at = grid_row(jnp.where(i < chunks.high[f], i, ROWS))
                for half in range(2):
                    stage[half, chunks.staged(i, f, j), :] = tables[f][half][at, :]
                return carry

            lax.fori_loop(first, last, copy_row, 0)
        if chunks.again:

            @pl.when(j == chunks.whole - 1)
            def _():
                stage[:, 2 * STRIDE : 2 * (STRIDE + chunks.again), :] = jnp.zeros((2, 2 * chunks.again, 128), F32)

        g = jnp.concatenate([stage[half, chunks.inner, :].astype(BF) for half in range(2)], 1)
        sum_ref[...] += dot_tn(m, g)

    chunks.run(reduce)
    for n in range(SHARDS):
        out_ref[place(ids_ref[2] ^ n, EARLY_SUM_BITS)] = sum_ref[n * RS : (n + 1) * RS].astype(BF)


def sample_backward(idx, size, ids, memory_t, ds_mine, ds_other, fa_mine, fa_other):
    return pl.pallas_call(
        scatter_kernel,
        in_specs=[ANY, SM, SM, ANY] + [VM] * 4,
        out_specs=VM,
        out_shape=jax.ShapeDtypeStruct((SHARDS, RS, D), BF),
        scratch_shapes=sampling_scratch(2, 3344) + [pltpu.VMEM((2, FR, D), BF)] + sampling_semaphores(2) + [pltpu.VMEM((D, D), F32)] + pick_scratch(),
        compiler_params=params(),
        cost_estimate=cost(30_000_000_000, 60_000_000),
        name="sample_backward",
    )(idx, size, ids, memory_t, ds_mine, ds_other, fa_mine, fa_other)
EPSILON = 1e-05
SMOOTHING = 1e-06
SCALE = (D // H) ** (-0.5)
GELU_C = 0.7978845608028654
GELU_K = 0.044715


def norm_forward(y, gain, shift):
    centred = y - jnp.mean(y, -1, keepdims=True)
    rstd = lax.rsqrt(jnp.mean(centred * centred, -1, keepdims=True) + EPSILON)
    unit = centred * rstd
    return unit * gain + shift, unit, rstd


def norm_backward(grad, unit, rstd, gain):
    d_gain = jnp.sum(grad * unit, 0, keepdims=True)
    d_shift = jnp.sum(grad, 0, keepdims=True)
    g = grad * gain
    dy = rstd * (g - jnp.mean(g, -1, keepdims=True) - unit * jnp.mean(g * unit, -1, keepdims=True))
    return dy, d_gain, d_shift


def gelu_pair(u):
    sq = u * u
    t = jnp.tanh(GELU_C * (u + GELU_K * u * sq))
    half = 0.5 * (1.0 + t)
    slope = half + 0.5 * u * (1.0 - t * t) * (GELU_C * (1.0 + 3.0 * GELU_K * sq))
    return u * half, slope


def head_rows():
    lane = lax.broadcasted_iota(jnp.int32, (1, D), 1) // (D // H)
    return [(lane == h).astype(F32).astype(BF) for h in range(H)]


def attend_forward(x, wq, wk, wv, wo, bias, p_ref):
    xb = x.astype(BF)
    q, k, v = (dot(xb, w).astype(BF) for w in (wq, wk, wv))
    live = lax.broadcasted_iota(jnp.int32, (FR, FR), 1) < Q
    mixed = None
    for h, mask in enumerate(head_rows()):
        s = jnp.where(live, dot_nt(q * mask, k) * SCALE, -1e30)
        e = jnp.exp(s - jnp.max(s, -1, keepdims=True))
        weights = (e / jnp.sum(e, -1, keepdims=True)).astype(BF)
        p_ref[h] = weights
        part = dot(weights, v * mask)
        mixed = part if mixed is None else mixed + part
    mixed = mixed.astype(BF)
    return x + dot(mixed, wo) + bias, xb, q, k, v, mixed


def attend_backward(dy, xb, q, k, v, mixed, p_ref, wq, wk, wv, wo):
    dyb = dy.astype(BF)
    d_wo = dot_tn(mixed, dyb)
    d_mixed = dot_nt(dyb, wo).astype(BF)
    dq = dk = dv = None
    for h, mask in enumerate(head_rows()):
        weights = p_ref[h]
        dm = d_mixed * mask
        dp = dot_nt(dm, v)
        w32 = weights.astype(F32)
        prod = w32 * dp
        ds = ((prod - w32 * jnp.sum(prod, -1, keepdims=True)) * SCALE).astype(BF)
        parts = (dot(ds, k * mask), dot_tn(ds, q * mask), dot_tn(weights, dm))
        dq, dk, dv = parts if dq is None else (dq + parts[0], dk + parts[1], dv + parts[2])
    dq, dk, dv = dq.astype(BF), dk.astype(BF), dv.astype(BF)
    dx = dy + dot_nt(dq, wq) + dot_nt(dk, wk) + dot_nt(dv, wv)
    return dx, (dot_tn(xb, dq), dot_tn(xb, dk), dot_tn(xb, dv), d_wo)


def group_spread(x, op):
    lane = lane_iota(x.shape[0])
    x = op(x, pltpu.roll(x, 64, 1))
    x = op(x, pltpu.roll(x, 32, 1))
    for step in (1, 2):
        other = jnp.where((lane & step) == 0, pltpu.roll(x, 128 - step, 1), pltpu.roll(x, step, 1))
        x = op(x, other)
    return x


LATE = 23 * RS // 2


def early_kernel(ids_ref, count_ref, square_ref, query_ref, vec_ref, out_ref):
    own, me = ids_ref[1], ids_ref[2]
    count = sum(count_ref[i] for i in range(count_ref.shape[0])).astype(F32)
    row, lane = lax.broadcasted_iota(jnp.int32, (24, RS), 0), jnp.zeros((24, 128 - RS), F32)
    vec = jnp.concatenate([vec_ref[...], jnp.zeros((3, RS), F32)], 0)
    vec = jnp.concatenate([jnp.where(row == 21, count, vec), lane], 1)
    vec = pltpu.roll(vec, me % 4 * RS, 1)
    zero = jnp.zeros_like(vec)
    vec = jnp.concatenate([jnp.where(me < 4, vec, zero), jnp.where(me < 4, zero, vec)], 1)
    first = square_ref[:4].reshape(4 * RS, D)
    right = jnp.concatenate([query_ref[: RS // 2, D:], query_ref[RS // 2 :, D:]], 1)
    second = jnp.concatenate([square_ref[4], query_ref[:, :D], right, vec, jnp.zeros((24, D), F32)], 0)
    out_ref[0] = jnp.where(own == 0, first, second).astype(BF)


def pack_early(ids, count, square, query, vec):
    return pl.pallas_call(
        early_kernel,
        grid=(1,),
        in_specs=[SM, SM, pl.BlockSpec((5, RS, D), lambda i: (0, 0, 0)), VM, VM],
        out_specs=VM,
        out_shape=jax.ShapeDtypeStruct((1, 128, D), BF),
        name="pack_early",
    )(ids, count, square, query, vec)


def late_kernel(ids_ref, square_ref, in_ref, out_weight_ref, out_ref, all_ref):
    for m in range(7):
        all_ref[m * RS : (m + 1) * RS] = square_ref[5 + m].astype(BF)
    for i in range(2):
        for c in range(4):
            row = (7 + 4 * i + c) * RS
            all_ref[row : row + RS] = in_ref[i, :, c * D : (c + 1) * D].astype(BF)
        all_ref[(15 + 4 * i) * RS : (19 + 4 * i) * RS] = out_weight_ref[i].astype(BF)
    out_ref[0] = all_ref[pl.ds(pl.multiple_of(ids_ref[1] * LATE, 16), LATE)]


def pack_late(ids, square, ffn_in, ffn_out):
    return pl.pallas_call(
        late_kernel,
        in_specs=[SM, VM, VM, VM],
        out_specs=VM,
        out_shape=jax.ShapeDtypeStruct((1, LATE, D), BF),
        scratch_shapes=[pltpu.VMEM((2 * LATE, D), BF)],
        name="pack_late",
    )(ids, square, ffn_in, ffn_out)


def order(bits):
    return [sum(bit for i, bit in enumerate(bits) if n >> i & 1) for n in range(SHARDS)]


def unpack_early(me, own, mine_ref, other_ref, w_ref, wq_ref, s4_ref, vec_ref):
    def take(first_ref, second_ref):
        rows = jnp.zeros((24, D), F32)
        for n in range(SHARDS):
            at = pl.ds(pl.multiple_of((me ^ order(EARLY_BITS)[n]) * RS, RS), RS)
            for m in range(4):
                w_ref[m, at, :] = first_ref[n, m * RS : (m + 1) * RS]
            s4_ref[at, :] = second_ref[n, :RS]
            wq_ref[at, :D] = second_ref[n, RS : 2 * RS]
            right = second_ref[n, 2 * RS : 2 * RS + RS // 2]
            wq_ref[at, D:] = jnp.concatenate([right[:, :128], right[:, 128:]], 0)
            rows = rows + second_ref[n, 2 * RS + RS // 2 : 128].astype(F32)[:24]
        vec_ref[...] = rows

    @pl.when(own == 0)
    def _():
        take(mine_ref, other_ref)

    @pl.when(own == 1)
    def _():
        take(other_ref, mine_ref)


def front_kernel(
    ids_ref, x_ref, mine_ref, other_ref,
    w_ref, wq_ref, s4_ref, vec_ref, total_ref, xb_ref, dec_ref, y_ref, q_ref, k_ref, v_ref, m_ref, p_ref, fa_ref, send_ref, att_ref,
):
    unpack_early(ids_ref[2], ids_ref[1], mine_ref, other_ref, w_ref, wq_ref, s4_ref, vec_ref)
    total_ref[...] = jnp.sum(vec_ref[21:22], -1, keepdims=True) / RS
    x = x_ref[...].astype(F32)
    x = jnp.where(ids_ref[1] == 0, x[:Q], x[Q:])
    x = jnp.concatenate([x, jnp.zeros((FR - Q, D), F32)], 0)
    y, xb_ref[...], q, k, v, mixed = attend_forward(x, w_ref[0], w_ref[1], w_ref[2], w_ref[3], vec_ref[10:11], p_ref)
    y_ref[...], q_ref[...], k_ref[...], v_ref[...], m_ref[...] = y, q, k, v, mixed
    dec, _, _ = norm_forward(y, vec_ref[0:1], vec_ref[1:2])
    dec_ref[...] = dec
    proj = dot(dec.astype(BF), wq_ref[...])
    fx, fy = jax.nn.sigmoid(proj[:, :128]), jax.nn.sigmoid(proj[:, 128:256])
    logits = proj[:, 256:]
    e = jnp.exp(logits - group_spread(logits, jnp.maximum))
    att = e / group_spread(e, jnp.add)
    att_ref[...] = att
    lane = lane_iota(FR)
    for out, back in ((fa_ref, ids_ref[0] * 32), (send_ref, (ids_ref[0] ^ 1) * 32)):
        out[...] = jnp.where(
            lane < 32,
            pltpu.roll(fx, 128 - back, 1),
            jnp.where(lane < 64, pltpu.roll(fy, 160 - back, 1), pltpu.roll(att, 192 - back, 1)),
        )


def frame_rows(dt, width=D):
    return jax.ShapeDtypeStruct((FR, width), dt)


WEIGHT_SHAPES = [
    jax.ShapeDtypeStruct((4, D, D), BF),
    jax.ShapeDtypeStruct((D, 384), BF),
    jax.ShapeDtypeStruct((D, D), BF),
    jax.ShapeDtypeStruct((24, D), F32),
    jax.ShapeDtypeStruct((1, 1), F32),
]
DENSE_LIMIT = 40 * 1024 * 1024


def front_forward(ids, x, mine, other):
    return pl.pallas_call(
        front_kernel,
        in_specs=[SM, VM, VM, VM],
        out_specs=[VM] * 16,
        out_shape=WEIGHT_SHAPES
        + [frame_rows(BF)]
        + [frame_rows(F32)] * 2
        + [frame_rows(BF)] * 4
        + [jax.ShapeDtypeStruct((H, FR, FR), BF)]
        + [frame_rows(F32, 128)] * 3,
        compiler_params=params(),
        cost_estimate=cost(1_000_000_000, 5_000_000),
        name="front_forward",
    )(ids, x, mine, other)


def front_back_kernel(
    ids_ref, near_ref, far_ref, att_ref, dres_ref, x_ref, dec_ref, y_ref, q_ref, k_ref, v_ref, m_ref, p_ref,
    w_ref, wq_ref, vec_ref, dpost_ref,
    mine_ref, send_ref, all_ref,
):
    me, own, level = ids_ref[2], ids_ref[1], ids_ref[0]
    lane = lane_iota(FR)
    cols = [None, None, None]
    for n, gp_ref in enumerate((near_ref.at[0], near_ref.at[1], far_ref.at[0], far_ref.at[1])):
        at = level ^ n
        gp = gp_ref[...].astype(F32)
        here = lane // 32 == at
        for part in range(3):
            piece = jnp.where(here, pltpu.roll(gp, (at + 4 - part) % 4 * 32, 1), 0.0)
            cols[part] = piece if cols[part] is None else cols[part] + piece
    weighted = cols[2]
    cols[2] = weighted - att_ref[...] * group_spread(weighted, jnp.add)
    grad = jnp.concatenate([c.astype(BF) for c in cols], 1)
    d_dec = dres_ref[...] + dot_nt(grad, wq_ref[...])
    _, unit, rstd = norm_forward(y_ref[...], vec_ref[0:1], vec_ref[1:2])
    dy, d_gain, d_shift = norm_backward(d_dec, unit, rstd, vec_ref[0:1])
    xb = x_ref[...]
    _, d_w = attend_backward(
        dy, xb, q_ref[...], k_ref[...], v_ref[...], m_ref[...], p_ref, w_ref[0], w_ref[1], w_ref[2], w_ref[3]
    )
    d_wq = dot_tn(dec_ref[...].astype(BF), grad)
    front = jnp.concatenate([d_gain, d_shift, jnp.zeros((8, D), F32), jnp.sum(dy, 0, keepdims=True), jnp.zeros((13, D), F32)], 0)
    d_vec = dpost_ref[...] + front
    d_w = [w.astype(BF) for w in d_w]
    d_wq = d_wq.astype(BF)
    d_vec = d_vec.astype(BF)
    first, second = own, 1 - own
    for shard in range(SHARDS):
        n = place(me ^ shard, EARLY_SUM_BITS)
        at = slice(shard * RS, (shard + 1) * RS)
        for m in range(4):
            all_ref[first, n, m * RS : (m + 1) * RS] = d_w[m][at]
        all_ref[second, n, :RS] = jnp.zeros((RS, D), BF)
        all_ref[second, n, RS : 2 * RS] = d_wq[at, :D]
        right = d_wq[at, D:]
        all_ref[second, n, 2 * RS : 2 * RS + RS // 2] = jnp.concatenate([right[: RS // 2], right[RS // 2 :]], 1)
        all_ref[second, n, 2 * RS + RS // 2 : 128] = jnp.concatenate([d_vec, jnp.zeros((24, D), BF)], 0)
    mine_ref[...] = all_ref[0]
    send_ref[...] = all_ref[1]


def front_backward(*args):
    half = jax.ShapeDtypeStruct((SHARDS, 128, D), BF)
    return pl.pallas_call(
        front_back_kernel,
        in_specs=[SM] + [VM] * 16,
        out_specs=[VM, VM],
        out_shape=[half, half],
        scratch_shapes=[pltpu.VMEM((2, SHARDS, 128, D), BF)],
        compiler_params=params(),
        cost_estimate=cost(2_000_000_000, 5_000_000),
        name="front_backward",
    )(*args)


def smooth_max(a, b):
    return 0.5 * (a + b + jnp.sqrt((a - b) * (a - b) + SMOOTHING))


def smooth_min(a, b):
    return 0.5 * (a + b - jnp.sqrt((a - b) * (a - b) + SMOOTHING))


def box_cost(p, t):
    distance = sum(jnp.sqrt((a - b) * (a - b) + 0.01) for a, b in zip(p, t))
    inter = hull = None
    for axis in range(2):
        p_low, p_up = p[axis] - 0.5 * p[axis + 2], p[axis] + 0.5 * p[axis + 2]
        t_low, t_up = t[axis] - 0.5 * t[axis + 2], t[axis] + 0.5 * t[axis + 2]
        over = smooth_max(smooth_min(p_up, t_up) - smooth_max(p_low, t_low), 0.0)
        enclose = smooth_max(p_up, t_up) - smooth_min(p_low, t_low)
        inter, hull = (over, enclose) if inter is None else (inter * over, hull * enclose)
    union = p[2] * p[3] + t[2] * t[3] - inter
    general = inter / union - (hull - union) / hull
    return 5.0 * distance + 2.0 * (1.0 - general)


LOSS_UNITS = [16.0 ** (3 - n) for n in range(8)]
def unpack_late(me, own, mine, other, ws_ref, fi_ref, fo_ref):
    def take(halves):
        for n in range(SHARDS):
            shard = me ^ order(LATE_BITS)[n]
            at = pl.ds(pl.multiple_of(shard * RS, RS), RS)

            def rows(block):
                parts = []
                for p in (block * RS, block * RS + RS // 2):
                    parts.append(halves[p // LATE][n // 4][n % 4, p % LATE : p % LATE + RS // 2])
                return jnp.concatenate(parts, 0)

            for m in range(7):
                ws_ref[m, at] = rows(m)
            for i in range(2):
                for c in range(4):
                    fi_ref[i, at, c * D : (c + 1) * D] = rows(7 + 4 * i + c)
                    down = pl.ds(pl.multiple_of((4 * shard + c) * RS, RS), RS)
                    fo_ref[i, down] = rows(15 + 4 * i + c)

    @pl.when(own == 0)
    def _():
        take((mine, other))

    @pl.when(own == 1)
    def _():
        take((other, mine))


def post_kernel(
    ids_ref, match_ref, count_ref, s_ref, add_ref, dec_ref, tgt_ref, late_a, late_b, late_c, late_d, vec_ref,
    ds_ref, dres_ref, mine_ref, send_ref, dvec_ref,
    ws_ref, fi_ref, fo_ref, all_ref, p_ref, box_ref, pick_ref,
):
    own = ids_ref[1]
    f = own
    me = ids_ref[2]
    unpack_late(me, own, (late_a, late_b), (late_c, late_d), ws_ref, fi_ref, fo_ref)
    dvec_ref[...] = jnp.zeros_like(dvec_ref)
    kept, given = own, 1 - own

    def put_square(m, grad):
        grad = grad.astype(BF)
        for n in range(SHARDS):
            all_ref[kept, place(me ^ n, LATE_SUM_BITS), m * RS : (m + 1) * RS] = grad[n * RS : (n + 1) * RS]

    def put_in(i, grad):
        grad = grad.astype(BF)
        for n in range(SHARDS):
            for c in range(4):
                piece = grad[n * RS : (n + 1) * RS, c * D : (c + 1) * D]
                if i == 0:
                    all_ref[kept, place(me ^ n, LATE_SUM_BITS), (7 + c) * RS : (8 + c) * RS] = piece
                else:
                    all_ref[given, place(me ^ n, LATE_SUM_BITS), c * RS : (c + 1) * RS] = piece

    def put_out(i, grad):
        grad = grad.astype(BF)
        for n in range(SHARDS):
            all_ref[given, place(me ^ n, LATE_SUM_BITS), (4 + 4 * i) * RS : (8 + 4 * i) * RS] = grad[n * 4 * RS : (n + 1) * 4 * RS]

    vec = lambda row: vec_ref[row : row + 1]
    total = lambda value: jnp.sum(value, 0, keepdims=True)

    def add_vec(row, value):
        dvec_ref[row : row + 1] += value

    sb = (s_ref[...].astype(F32) + add_ref[...].astype(F32)).astype(BF)
    first, unit2, rstd2 = norm_forward(dec_ref[...] + dot(sb, ws_ref[0]) + vec(11), vec(2), vec(3))
    firstb = first.astype(BF)
    hid1, slope1 = gelu_pair(dot(firstb, fi_ref[0]))
    hid1 = hid1.astype(BF)
    second, unit3, rstd3 = norm_forward(first + dot(hid1, fo_ref[0]) + vec(12), vec(4), vec(5))
    y4, secondb, q, k, v, mixed = attend_forward(second, ws_ref[1], ws_ref[2], ws_ref[3], ws_ref[4], vec(13), p_ref)
    third, unit4, rstd4 = norm_forward(y4, vec(6), vec(7))
    thirdb = third.astype(BF)
    hid2, slope2 = gelu_pair(dot(thirdb, fi_ref[1]))
    hid2 = hid2.astype(BF)
    fourth, unit5, rstd5 = norm_forward(third + dot(hid2, fo_ref[1]) + vec(14), vec(8), vec(9))
    fourthb = fourth.astype(BF)
    z1, slope_z1 = gelu_pair(dot(fourthb, ws_ref[5]) + vec(15))
    z1 = z1.astype(BF)
    z2, slope_z2 = gelu_pair(dot(z1, ws_ref[6]) + vec(16))
    z2 = z2.astype(BF)
    w3 = jnp.concatenate([vec_ref[17:21], jnp.zeros((124, D), F32)], 0).astype(BF)
    boxes = jax.nn.sigmoid(dot_nt(z2, w3))
    box_ref[...] = boxes
    slots = tgt_ref.shape[1]
    for o in range(slots):
        pick_ref[o : o + 1, :] = box_ref[pl.ds(match_ref[f, o], 1), :]
    picked = pick_ref[...]
    pred = [picked[:, c : c + 1] for c in range(4)]
    target = [tgt_ref[own, :, c : c + 1] for c in range(4)]
    valid = (lax.broadcasted_iota(jnp.int32, (slots, 1), 0) < count_ref[f]).astype(F32)
    price, pull = jax.vjp(lambda *p: box_cost(p, target), *pred)
    loss = jnp.sum(valid * price, 0, keepdims=True)
    count = jnp.sum(vec_ref[21:22], -1, keepdims=True) / RS
    d_pred = pull(valid / count)
    lane = lane_iota(slots)
    rows = jnp.zeros((slots, 128), F32)
    for c in range(4):
        rows = jnp.where(lane == c, d_pred[c], rows)
    pick_ref[...] = rows
    box_ref[...] = jnp.zeros((FR, 128), F32)
    for o in range(slots):
        box_ref[pl.ds(match_ref[f, o], 1), :] = pick_ref[o : o + 1, :]
    d_logit = (box_ref[...] * boxes * (1.0 - boxes)).astype(BF)
    dvec_ref[17:21] += dot_tn(d_logit, z2)[0:4]
    du = dot(d_logit, w3) * slope_z2
    add_vec(16, total(du))
    du = du.astype(BF)
    put_square(6, dot_tn(z1, du))
    du = dot_nt(du, ws_ref[6]) * slope_z1
    add_vec(15, total(du))
    du = du.astype(BF)
    put_square(5, dot_tn(fourthb, du))
    grad = dot_nt(du, ws_ref[5])

    def ffn_back(grad, unit, rstd, i, row, bias, hid, slope, inputb):
        dy, d_gain, d_shift = norm_backward(grad, unit, rstd, vec(row))
        add_vec(row, d_gain)
        add_vec(row + 1, d_shift)
        add_vec(bias, total(dy))
        dyb = dy.astype(BF)
        put_out(i, dot_tn(hid, dyb))
        du = (dot_nt(dyb, fo_ref[i]) * slope).astype(BF)
        put_in(i, dot_tn(inputb, du))
        return dy + dot_nt(du, fi_ref[i])

    grad = ffn_back(grad, unit5, rstd5, 1, 8, 14, hid2, slope2, thirdb)
    dy, d_gain, d_shift = norm_backward(grad, unit4, rstd4, vec(6))
    add_vec(6, d_gain)
    add_vec(7, d_shift)
    add_vec(13, total(dy))
    grad, d_w = attend_backward(dy, secondb, q, k, v, mixed, p_ref, ws_ref[1], ws_ref[2], ws_ref[3], ws_ref[4])
    for i in range(4):
        put_square(1 + i, d_w[i])
    grad = ffn_back(grad, unit3, rstd3, 0, 4, 12, hid1, slope1, firstb)
    dy, d_gain, d_shift = norm_backward(grad, unit2, rstd2, vec(2))
    add_vec(2, d_gain)
    add_vec(3, d_shift)
    add_vec(11, total(dy))
    dres_ref[...] = dy
    dyb = dy.astype(BF)
    put_square(0, dot_tn(sb, dyb))
    ds_ref[...] = dot_nt(dyb, ws_ref[0]).astype(BF)
    row = lax.broadcasted_iota(jnp.int32, (RS, D), 0)
    rows, above = jnp.zeros((RS, D), F32), jnp.zeros((1, 1), F32)
    for n, unit in enumerate(LOSS_UNITS):
        whole = jnp.floor(loss * (1.0 / unit))
        rows = jnp.where(row == n, whole - 16.0 * above, rows)
        above = whole
    rows = rows.astype(BF)
    for n in range(SHARDS):
        all_ref[kept, place(me ^ n, LATE_SUM_BITS), 11 * RS : 12 * RS] = rows
    mine_ref[...] = all_ref[0]
    send_ref[...] = all_ref[1]


def post_step(ids, match, count, half, add, dec, target, late, vec):
    half_rows = jax.ShapeDtypeStruct((SHARDS, 12 * RS, D), BF)
    return pl.pallas_call(
        post_kernel,
        in_specs=[SM, SM, SM] + [VM] * 9,
        out_specs=[VM] * 5,
        out_shape=[frame_rows(BF), frame_rows(F32), half_rows, half_rows, jax.ShapeDtypeStruct((24, D), F32)],
        scratch_shapes=[
            pltpu.VMEM((7, D, D), BF),
            pltpu.VMEM((2, D, 4 * D), BF),
            pltpu.VMEM((2, 4 * D, D), BF),
            pltpu.VMEM((2, SHARDS, 12 * RS, D), BF),
            pltpu.VMEM((H, FR, FR), BF),
            pltpu.VMEM((FR, 128), F32),
            pltpu.VMEM((target.shape[1], 128), F32),
        ],
        compiler_params=params(DENSE_LIMIT),
        cost_estimate=cost(8_000_000_000, 10_000_000),
        name="post_step",
    )(ids, match, count, half, add, dec, target, *late, vec)


LEARNING_RATE = 2.0
MOMENTUM = 0.5
AVERAGING = 0.5


def update(master, gradient, moment, average):
    moment_new = MOMENTUM * moment + gradient
    master_new = master - LEARNING_RATE * (gradient + MOMENTUM * moment_new)
    average_new = AVERAGING * average + (1.0 - AVERAGING) * master_new
    return (master_new, master_new.astype(BF), moment_new, average_new)


def apply_kernel(ids_ref, last_mine, last_other, late_mine, late_other, *refs):
    own, me = ids_ref[1], ids_ref[2]
    masters, moments, averages, loss_ref, outs = refs[:5], refs[5:10], refs[10:15], refs[15], refs[16:]

    def halves(mine, other):
        mine, other = mine[...], other[...]
        return jnp.where(own == 0, mine, other), jnp.where(own == 0, other, mine)

    last, late = halves(last_mine, last_other), halves(late_mine, late_other)

    def step(which, index, grad):
        new = update(masters[which][index], grad, moments[which][index], averages[which][index])
        for out, value in zip(outs[4 * which : 4 * which + 4], new):
            out[index] = value

    def block(rows, n, count=1):
        return rows[n * RS : (n + count) * RS]

    step(0, (slice(None), slice(0, D)), block(last[1], 1))
    right = last[1][2 * RS : 2 * RS + RS // 2]
    step(0, (slice(0, RS // 2), slice(D, D + 128)), right[:, :128])
    step(0, (slice(RS // 2, RS), slice(D, D + 128)), right[:, 128:])
    for m in range(12):
        step(1, (m,), block(last[0], m) if m < 4 else block(last[1], 0) if m == 4 else block(late[0], m - 5))
    for i in range(2):
        for c in range(4):
            step(2, (i, slice(None), slice(c * D, (c + 1) * D)), block(late[1], c) if i else block(late[0], 7 + c))
        step(3, (i,), block(late[1], 4 + 4 * i, 4))
    vec = last[1][2 * RS + RS // 2 : 2 * RS + RS // 2 + 24]
    vec = jnp.where(me >= 4, vec[:, 128:], vec[:, :128])
    vec = pltpu.roll(vec, (4 - me % 4) % 4 * RS, 1)
    step(4, (slice(None), slice(None)), vec[:21, :RS])
    loss_ref[...] = sum(late[0][11 * RS + n : 11 * RS + n + 1, 0:1] * unit for n, unit in enumerate(LOSS_UNITS))


def apply_updates(ids, grads, masters, moments, averages):
    shapes = [jax.ShapeDtypeStruct((1, 1), F32)]
    for master in masters:
        full = jax.ShapeDtypeStruct(master.shape, F32)
        shapes += [full, jax.ShapeDtypeStruct(master.shape, BF), full, full]
    loss, *outs = pl.pallas_call(
        apply_kernel,
        in_specs=[SM] + [VM] * 19,
        out_specs=[VM] * 21,
        out_shape=shapes,
        compiler_params=params(24 * 1024 * 1024),
        cost_estimate=cost(3_000_000, 8_000_000),
        name="apply_updates",
    )(ids, *grads, *masters, *moments, *averages)
    return loss.reshape(()), outs


def pairs(size, bit):
    return [(i, i ^ bit) for i in range(size)]


def swap_core(value):
    return lax.ppermute(value, "level", pairs(4, 1))


def swap_chip(value):
    return lax.ppermute(value, "level", pairs(4, 2))


def pick(pair, index):
    return lax.dynamic_index_in_dim(pair, index, 0, keepdims=False)


def in_order(mine, other, index):
    return jnp.where(index == 0, mine, other), jnp.where(index == 0, other, mine)


def after(value, event):
    return lax.optimization_barrier((value, event))[0]


def early_rows(square, query, vec):
    right = jnp.concatenate([query[: RS // 2, D:], query[RS // 2 :, D:]], 1)
    second = jnp.concatenate([square[4], query[:, :D], right, vec, jnp.zeros((24, D), vec.dtype)], 0)
    return jnp.stack([square[:4].reshape(4 * RS, D), second])


def late_rows(square, ffn_in, ffn_out):
    return jnp.concatenate(
        [
            square.reshape(7 * RS, D),
            ffn_in.reshape(2, RS, 4, D).transpose(0, 2, 1, 3).reshape(8 * RS, D),
            ffn_out.reshape(8 * RS, D),
        ],
        0,
    )


def gather_weights(dp, ids, own, rows, w_query, w_square, w_ffn_in, w_ffn_out, vectors, counts):
    if dp == SHARDS:
        early = pack_early(ids, counts, w_square, w_query, vectors)
        early, *late = lax.optimization_barrier((early, w_square, w_ffn_in, w_ffn_out))
        first = lax.ppermute(early, "dp", pairs(dp, EARLY_BITS[0]))
        late = pack_late(ids, *late)
        early, late, rows = lax.optimization_barrier((jnp.concatenate([early, first], 0), late, rows))
        second = lax.ppermute(early, "dp", pairs(dp, EARLY_BITS[1]))
        late_first = lax.ppermute(late, "dp", pairs(dp, LATE_BITS[0]))
        early, late_first = lax.optimization_barrier((jnp.concatenate([early, second], 0), late_first))
        third = lax.ppermute(early, "dp", pairs(dp, EARLY_BITS[2]))
        late = jnp.concatenate([late, after(late_first, third)], 0)
        late = (late, lax.ppermute(late, "dp", pairs(dp, LATE_BITS[1])))
        early = jnp.concatenate([early, third], 0)
        return rows, early, swap_core(early), late

    rs = D // dp
    here = jnp.arange(D, dtype=jnp.int32)[None, :] // rs == lax.axis_index("dp")
    vec = jnp.where(here, jnp.tile(jnp.pad(vectors, ((0, 3), (0, 0))), (1, dp)), 0.0)
    vec = jnp.where(here & (jnp.arange(24)[:, None] == 21), jnp.sum(counts).astype(F32), vec)

    def whole(weight, dim):
        return lax.all_gather(weight.astype(BF), "dp", axis=dim, tiled=True)

    square, query = whole(w_square, 1), whole(w_query, 0)
    ffn_in, ffn_out = whole(w_ffn_in, 1), whole(w_ffn_out, 1)
    vec = lax.psum(vec, "dp")
    early, late = [], []
    for n in order(EARLY_BITS):
        at = slice(n * RS, (n + 1) * RS)
        columns = jnp.where(jnp.arange(D)[None, :] // RS == n, vec, 0.0).astype(BF)
        early.append(early_rows(square[:5, at], query[at], columns))
    for n in order(LATE_BITS):
        at = slice(n * RS, (n + 1) * RS)
        late.append(late_rows(square[5:, at], ffn_in[:, at], ffn_out[:, 4 * n * RS : 4 * (n + 1) * RS]))
    early = jnp.stack(early, 1)
    late = pick(jnp.stack(late).reshape(SHARDS, 2, -1, D).transpose(1, 0, 2, 3), own).reshape(2, 4, -1, D)
    return rows, pick(early, own), pick(early, 1 - own), late


def halve(value):
    count = value.shape[0] // 2
    return value[:count], value[count:].astype(BF)


def send(value, bit):
    return lax.ppermute(value, "dp", pairs(SHARDS, bit))


def shards(
    queries, memory, frame_size, sample_pick, target_box, match, obj_count,
    w_query, w_square, w_ffn_in, w_ffn_out, vectors,
    m_query, m_square, m_ffn_in, m_ffn_out, m_vectors,
    a_query, a_square, a_ffn_in, a_ffn_out, a_vectors,
):
    dp = lax.axis_size("dp")
    rs = D // dp
    shard = lax.axis_index("dp")
    level = lax.axis_index("level")
    own = level % 2
    me = shard if dp == SHARDS else 0
    ids = jnp.stack([level, own, me, 0]).astype(jnp.int32)
    rows = pick_rows(frame_size, ids, sample_pick[:, 0, :].T)
    rows, mine, other, late = gather_weights(
        dp, ids, own, rows, w_query, w_square, w_ffn_in, w_ffn_out, vectors, obj_count
    )
    memory_t = memory.transpose(1, 2, 0, 3)
    w4, wq, s4, vec, total, x, dec, y, q, k, v, mixed, p, fa, fa_send, att = front_forward(ids, queries, mine, other)
    fa_other = swap_core(fa_send)
    if dp == SHARDS:
        late = jnp.concatenate([late[0], after(late[1], att)], 0)
        s4 = after(s4, late)
        late = (late, lax.ppermute(late, "dp", pairs(dp, LATE_BITS[2])))
    gathered, part, part_send = sample_forward(rows, frame_size, ids, memory_t, s4, fa, fa_other)
    part_other = swap_core(part_send)
    half = (part.astype(F32) + part_other.astype(F32)).astype(BF)
    half_other = swap_chip(half)
    late_end = after(late[1], half)
    late = (late[0], late_end, swap_core(late[0]), swap_core(late_end))
    ds, dres, late_mine, late_send, dvec = post_step(
        ids, match, obj_count, half, half_other, dec, target_box, late, vec
    )
    ds_other = swap_core(ds)
    late_sent = swap_core(after(late_send, ds_other))
    gp, gp_send = coef_backward(ids, gathered, ds, ds_other, fa, fa_other)
    near = jnp.stack([gp, swap_core(gp_send)])
    far = swap_chip(near)
    if dp == SHARDS:
        (keep, out), (keep_other, out_other) = halve(late_mine), halve(late_sent)
        late_kept = keep.astype(F32) + keep_other.astype(F32)
        late_out = (out.astype(F32) + out_other.astype(F32)).astype(BF)
        near, late_out, ds_other = lax.optimization_barrier((near, late_out, ds_other))
        late_in = send(late_out, LATE_SUM_BITS[0])
    else:
        late_sum = late_mine.astype(F32) + late_sent.astype(F32)
    d_s4 = sample_backward(rows, frame_size, ids, memory_t, ds, ds_other, fa, fa_other)
    if dp == SHARDS:
        far, late_in, d_s4 = lax.optimization_barrier((far, late_in, d_s4))
        late_kept, late_out = halve(late_kept + late_in.astype(F32))
        near, late_out = lax.optimization_barrier((near, late_out))
        late_in = send(late_out, LATE_SUM_BITS[1])
    d_s4_other = swap_chip(d_s4)
    last_mine, last_send = front_backward(
        ids, near, far, att, dres, x, dec, y, q, k, v, mixed, p, w4, wq, vec, dvec
    )
    d_s4 = (d_s4.astype(F32) + after(d_s4_other, last_mine).astype(F32)).astype(BF)
    d_s4 = jnp.where(own == 1, d_s4.astype(F32) + swap_core(d_s4).astype(F32), 0.0)
    last = last_mine.astype(F32) + swap_core(last_send).astype(F32)
    last = jnp.concatenate([last[:, :RS] + d_s4, last[:, RS:]], 1)
    if dp == SHARDS:
        late_kept, late_out = halve(late_kept + after(late_in, last_mine).astype(F32))
        last, late_out = lax.optimization_barrier((last, late_out))
        late_in = send(late_out, LATE_SUM_BITS[2])
        for bit in EARLY_SUM_BITS:
            if bit == EARLY_SUM_BITS[1]:
                last, late_in = lax.optimization_barrier((last, late_in))
            last_kept, last_out = halve(last)
            last = last_kept + send(last_out, bit).astype(F32)
        late_sum = (late_kept + late_in.astype(F32))[0]
        last = last[0]
    masters = (w_query, w_square, w_ffn_in, w_ffn_out, vectors)
    moments = (m_query, m_square, m_ffn_in, m_ffn_out, m_vectors)
    averages = (a_query, a_square, a_ffn_in, a_ffn_out, a_vectors)
    last_other, late_other = swap_core(last), swap_core(late_sum)
    if dp == SHARDS:
        loss, outs = apply_updates(ids, (last, last_other, late_sum, late_other), masters, moments, averages)
    else:
        last, late = in_order(last, last_other, own), in_order(late_sum, late_other, own)
        last = [jnp.stack([x[place(n, EARLY_SUM_BITS)] for n in range(SHARDS)]) for x in last]
        late = [jnp.stack([x[place(n, LATE_SUM_BITS)] for n in range(SHARDS)]) for x in late]
        loss = lax.psum(late[0][0, 11 * RS : 11 * RS + 8, 0], "dp")

        def square(rows):
            return rows.reshape(SHARDS, -1, RS, D).transpose(1, 0, 2, 3).reshape(-1, D, D)

        right = last[1][:, 2 * RS : 2 * RS + RS // 2].reshape(SHARDS, RS // 2, 2, 128).transpose(0, 2, 1, 3)
        g_query = jnp.concatenate([square(last[1][:, RS : 2 * RS])[0], right.reshape(D, 128)], 1)
        g_vec = last[1][0, 2 * RS + RS // 2 : 2 * RS + RS // 2 + 21]
        g_square = jnp.concatenate([square(last[0]), square(last[1][:, :RS]), square(late[0][:, : 7 * RS])], 0)
        g_in = [x.reshape(SHARDS, 4, RS, D).transpose(0, 2, 1, 3) for x in (late[0][:, 7 * RS : 11 * RS], late[1][:, : 4 * RS])]
        g_in = jnp.concatenate([x.reshape(1, D, 4 * D) for x in g_in], 0)
        g_out = late[1][:, 4 * RS :].reshape(SHARDS, 2, 4 * RS, D).transpose(1, 0, 2, 3).reshape(2, 4 * D, D)

        def scatter(grad, dim):
            return lax.psum_scatter(grad, "dp", scatter_dimension=dim, tiled=True)

        g_query, g_square, g_vec = scatter(g_query, 0), scatter(g_square, 1), scatter(g_vec, 1)
        g_in, g_out = scatter(g_in, 1), scatter(g_out, 1)
        grads = (g_query, g_square, g_in, g_out, g_vec)
        outs = [out for group in zip(masters, grads, moments, averages) for out in update(*group)]
        loss = jnp.sum(loss * jnp.array(LOSS_UNITS, F32))
    return (loss, total.reshape(()), *outs)


def solution(mesh):
    rows, mid, low = P("dp", None), P(None, "dp", None), P(None, "dp")
    five = (rows, mid, mid, mid, low)
    return jax.shard_map(
        shards,
        mesh=mesh,
        in_specs=(
            rows,
            P("dp", "level", None, None),
            rows,
            P("dp", "level", None),
            P("dp", None, None),
            rows,
            P("dp"),
        )
        + five * 3,
        out_specs=(P(), P()) + tuple(spec for spec in five for _ in range(4)),
        check_vma=False,
    )
```
